32 devices in a mesh: wide: 8 (over z, y), narrow: 4 (over x, core).
Axes of the slice: x: 2, y: 2, z: 4, core: 2. Of those that a mesh axis runs over, the one named last changes fastest.
Arguments:
- adjoint: float32 [3, 512, 256, 256], P(None, 'wide', 'narrow'), may hold values from -6 to 6
- velocity: float32 [3, 512, 256, 256], P(None, 'wide', 'narrow'), may hold values from -6 to 6
- deriv_x: float32 [256, 256], replicated, as said below
- deriv_y: float32 [256, 256], replicated, as said below
- deriv_z: float32 [512, 512], replicated, as said below
- rotor_blocks: int32 [96, 128], replicated, may hold values from 0 to 262143, as said below
- turbine_owner: int32 [96], replicated, may hold values from 0 to 31, as said below
- disk_weight: float32 [96, 128, 128], replicated, may hold values from 0.1 to 1
- thrust: float32 [96], replicated, may hold values from 0.5 to 2
Outputs:
- updated_adjoint: float32 [3, 512, 256, 256], P(None, 'wide', 'narrow')
- turbine_grad: float32 [128, 2], P(('wide', 'narrow'))
The draws below stay inside these ranges and needn't reach their ends.
Inputs may be any that keep to these rules, and one draw needn't show every extreme that they name: `deriv_x`: entries vanish where the row's block of 64 and the column's block differ by more than one. `deriv_y`: entries vanish where the row's block of 32 and the column's block differ by more than one. `deriv_z`: entries vanish where the row's block of 16 and the column's block differ by more than one. `rotor_blocks`: block id b = (z * 256 + y) * 2 + x block. A rotor's row lists 128 // 2 consecutive z planes times 2 consecutive y lines, all at one x block, z major. `turbine_owner`: devices are numbered wide major over wide and narrow. No device owns more than 4 turbines, and one owns exactly 4.
All inputs are finite; a program needn't handle non-finite values.
Results may differ from the reference program's by a relative error of at most 0.00014.
Values sent between devices are 32-bit elements; how exact they have to be, the bound alone decides.
A program may use at most 256 MiB of HBM per device.

```python
import math
import jax
import jax.numpy as jnp
from jax import lax

NX = 256
NY = 256
NZ = 512
BX = 64
BY = 32
BAND = 16
RY = 2
TURB = 96
ROTOR = 128
SLOTS = 4
DEVICES = 32


def band_matrix(key, order, block):
    row_block = jnp.arange(order)[:, None] // block
    col_block = jnp.arange(order)[None, :] // block
    in_band = (jnp.abs(row_block - col_block) <= 1).astype(jnp.float32)
    values = jax.random.normal(key, (order, order), jnp.float32)
    return values * in_band / jnp.sqrt(3.0 * block)


def draw_deriv_x(key, part):
    return band_matrix(jax.random.fold_in(key, 11), NX, BX)


def draw_deriv_y(key, part):
    return band_matrix(jax.random.fold_in(key, 12), NY, BY)


def draw_deriv_z(key, part):
    return band_matrix(jax.random.fold_in(key, 13), NZ, BAND)


def draw_rotor_blocks(key, part):
    key_z, key_y, key_x = jax.random.split(jax.random.fold_in(key, 21), 3)
    extent_z = ROTOR // RY
    x_blocks = NX // 128
    turbine = jnp.arange(TURB)
    start_z = jax.random.randint(key_z, (TURB,), 0, NZ - extent_z + 1)
    start_y = jax.random.randint(key_y, (TURB,), 0, NY - RY + 1)
    start_x = jax.random.randint(key_x, (TURB,), 0, x_blocks)
    start_z = jnp.where(turbine == 0, 0, jnp.where(turbine == 1, NZ - extent_z, start_z))
    start_y = jnp.where(turbine == 0, 0, jnp.where(turbine == 1, NY - RY, start_y))
    start_x = jnp.where(turbine == 0, 0, jnp.where(turbine == 1, x_blocks - 1, start_x))
    offset_z = jnp.arange(ROTOR) // RY
    offset_y = jnp.arange(ROTOR) % RY
    blocks = ((start_z[:, None] + offset_z[None, :]) * NY + start_y[:, None] + offset_y[None, :]) * x_blocks + start_x[:, None]
    return blocks.astype(jnp.int32)


def place_value(shuffled, wanted, target_slot):
    found_at = jnp.argmax((shuffled == wanted).astype(jnp.int32))
    previous = shuffled[target_slot]
    return shuffled.at[found_at].set(previous).at[target_slot].set(wanted)


def draw_turbine_owner(key, part):
    shuffled = jax.random.permutation(jax.random.fold_in(key, 31), DEVICES).astype(jnp.int32)
    shuffled = place_value(shuffled, 0, 2)
    shuffled = place_value(shuffled, DEVICES - 1, 1)
    turbine = jnp.arange(TURB)
    pick_index = jnp.where(turbine == TURB - 1, 0, turbine % DEVICES)
    return shuffled[pick_index].astype(jnp.int32)


def shard_levels(stream_key, extent, cuts, smallest, top_value):
    loudness, own = 1.0, jax.random.fold_in(stream_key, 6)
    for axis_at, shards_of in cuts:
        steps = jnp.exp(jax.random.uniform(jax.random.fold_in(own, axis_at), (shards_of,), jnp.float32, smallest / len(cuts), top_value / len(cuts)))
        loudness = loudness * jnp.repeat(steps, extent[axis_at] // shards_of).reshape([-1 if axis == axis_at else 1 for axis in range(len(extent))])
    return loudness


def gaussian(stream_key, shape, deviation, bound, cuts=(), kind=jnp.bfloat16):
    values = jax.random.normal(stream_key, shape, jnp.float32) * deviation
    if len(cuts) > 0:
        values = shard_levels(stream_key, shape, cuts, -0.22, 0.18) * values
    return jnp.clip(values, min=-bound, max=bound).astype(kind)


def setup_inputs(seed: int = 0) -> dict:
    key_list = jax.random.split(jax.random.key(seed), 10)
    adjoint = gaussian(key_list[0], (3, NZ, NY, NX), 1.0, 6.0, ((1, 8), (2, 4)), jnp.float32)
    velocity = gaussian(key_list[1], (3, NZ, NY, NX), 1.0, 6.0, ((1, 8), (2, 4)), jnp.float32)
    deriv_x = draw_deriv_x(jax.random.fold_in(key_list[9], 71), 0)
    deriv_y = draw_deriv_y(jax.random.fold_in(key_list[9], 71), 0)
    deriv_z = draw_deriv_z(jax.random.fold_in(key_list[9], 71), 0)
    rotor_blocks = draw_rotor_blocks(jax.random.fold_in(key_list[9], 71), 0)
    turbine_owner = draw_turbine_owner(jax.random.fold_in(key_list[9], 71), 0)
    disk_weight = jnp.clip(jnp.exp(jax.random.uniform(key_list[7], (TURB, ROTOR, 128), jnp.float32, math.log(0.1), math.log(1.0))), 0.1, 1.0)
    thrust = jnp.clip(jax.random.uniform(key_list[8], (TURB,), jnp.float32, 0.5, 2.0), 0.5, 2.0)
    return dict(adjoint=adjoint, velocity=velocity, deriv_x=deriv_x, deriv_y=deriv_y, deriv_z=deriv_z, rotor_blocks=rotor_blocks, turbine_owner=turbine_owner, disk_weight=disk_weight, thrust=thrust)


def directional(adjoint, velocity, adj_deriv, vel_deriv, direction):
    advect = velocity[direction][None] * adj_deriv
    stretch = -lax.optimization_barrier(jnp.sum(adjoint * vel_deriv, axis=0))
    select = (jnp.arange(3) == direction).astype(jnp.float32)[:, None, None, None]
    return advect + select * stretch[None]

def reference(adjoint, velocity, deriv_x, deriv_y, deriv_z, rotor_blocks, turbine_owner, disk_weight, thrust):
    highest = lax.Precision.HIGHEST
    tendency = jnp.zeros_like(adjoint)
    forms = (('czyk,xk->czyx', deriv_x), ('czkx,yk->czyx', deriv_y), ('ckyx,zk->czyx', deriv_z))
    for direction in range(3):
        form, matrix = forms[direction]
        adj_deriv = jnp.einsum(form, adjoint, matrix, precision=highest)
        vel_deriv = jnp.einsum(form, velocity, matrix, precision=highest)
        tendency = tendency + directional(adjoint, velocity, adj_deriv, vel_deriv, direction)
    x_blocks = NX // 128
    weighted = thrust[:, None, None] * disk_weight
    source = jnp.zeros((NZ * NY * x_blocks, 128), jnp.float32)
    source = source.at[rotor_blocks.reshape(-1)].add(weighted.reshape(-1, 128)).reshape(NZ, NY, NX)
    forcing = source * jnp.abs(velocity[0]) * adjoint[0]
    select = (jnp.arange(3) == 0).astype(jnp.float32)[:, None, None, None]
    tendency = tendency - select * forcing[None]
    updated = adjoint + 0.2 * tendency
    ax_rows = adjoint[0].reshape(-1, 128)[rotor_blocks]
    ay_rows = adjoint[1].reshape(-1, 128)[rotor_blocks]
    ux_rows = velocity[0].reshape(-1, 128)[rotor_blocks]
    thrust_drive = ux_rows * jnp.abs(ux_rows)
    scale = 1.0 / math.sqrt(128.0 * ROTOR)
    grad_thrust = lax.optimization_barrier(jnp.sum(disk_weight * ax_rows * thrust_drive, axis=(1, 2))) * scale
    grad_side = lax.optimization_barrier(jnp.sum(disk_weight * ay_rows * thrust_drive, axis=(1, 2))) * scale
    grad = jnp.stack([grad_thrust, grad_side], axis=1)
    positions = jnp.arange(TURB)
    shared = turbine_owner[:, None] == turbine_owner[None, :]
    earlier = positions[:, None] > positions[None, :]
    slot_rank = lax.optimization_barrier(jnp.sum((shared & earlier).astype(jnp.int32), axis=1)).astype(jnp.int32)
    target_slot = (turbine_owner * SLOTS + slot_rank).astype(jnp.int32)
    turbine_grad = jnp.zeros((DEVICES * SLOTS, 2), jnp.float32).at[target_slot].set(grad)
    return (updated, turbine_grad)
```

```python
import functools
import math

import jax
import jax.numpy as jnp
from jax import lax
from jax.experimental import pallas as pl
from jax.experimental.pallas import tpu as pltpu
from jax.sharding import PartitionSpec as P

NY = 256
BY = 32
BAND = 16
RY = 2
STEP = 0.2
GROUP = 8
VMEM = 56 * 1024 * 1024


def params():
    return pltpu.CompilerParams(vmem_limit_bytes=VMEM)


def cost(flops, moved):
    return pl.CostEstimate(flops=int(flops), bytes_accessed=int(moved), transcendentals=0)


def split(value):
    high = value.astype(jnp.bfloat16)
    low = (value - high.astype(jnp.float32)).astype(jnp.bfloat16)
    return high, low


def dot(left, right):
    return jnp.dot(left, right, preferred_element_type=jnp.float32)


def split_matrix(matrix):
    high = lax.reduce_precision(matrix, 8, 7)
    return high, matrix - high


def stacked(matrix):
    high, low = split_matrix(matrix)
    top = jnp.concatenate([high, high], axis=1)
    bottom = jnp.concatenate([low, jnp.zeros_like(low)], axis=1)
    return jnp.concatenate([top, bottom], axis=0).astype(jnp.bfloat16)


def paired(matrix, axis):
    high, low = split_matrix(matrix)
    return jnp.concatenate([high, low], axis=axis).astype(jnp.bfloat16)


def apply_stacked(matrix, values):
    product = dot(matrix, jnp.concatenate(split(values), axis=0))
    rows = product.shape[0] // 2
    return product[:rows] + product[rows:]


def turbine_kernel(
    count, shard, zs, ys, xs, thrust, a0, a1, u0, weight, source, grad0, grad1
):
    shard_z, shard_y, planes = shard
    step = pl.program_id(0)

    @pl.when(step == 0)
    def _():
        source[...] = jnp.zeros_like(source)

    grad0[...] = jnp.zeros_like(grad0)
    grad1[...] = jnp.zeros_like(grad1)
    for slot in range(count):
        turbine = step * count + slot
        first_z = zs[turbine]
        low = jnp.maximum(first_z, 0)
        high = jnp.minimum(first_z + planes, shard_z)
        lanes = pl.ds(pl.multiple_of(xs[turbine] * 128, 128), 128)
        for line in range(RY):
            y = ys[turbine] + line

            @pl.when((y >= 0) & (y < shard_y) & (high > low))
            def _():
                tile = pl.ds(pl.multiple_of(y // 8 * 8, 8), 8)
                chosen = lax.broadcasted_iota(jnp.int32, (8, 128), 0) == y % 8

                def body(z, sums):
                    row = weight[slot, pl.ds((z - first_z) * RY + line, 1), :]
                    row = jnp.where(chosen, jnp.broadcast_to(row, (8, 128)), 0.0)
                    at = (z, tile, lanes)
                    u = u0[at]
                    driven = row * u * jnp.abs(u)
                    source[at] += row * thrust[turbine]
                    return sums[0] + driven * a0[at], sums[1] + driven * a1[at]

                zero = jnp.zeros((8, 128), jnp.float32)
                sums = lax.fori_loop(low, high, body, (zero, zero))
                grad0[slot : slot + 1, :] += jnp.sum(sums[0], axis=0, keepdims=True)
                grad1[slot : slot + 1, :] += jnp.sum(sums[1], axis=0, keepdims=True)


def turbine_terms(adjoint, velocity, rotor_blocks, disk_weight, thrust):
    _, shard_z, shard_y, extent = adjoint.shape
    x_blocks = extent // 128
    turbines, blocks = rotor_blocks.shape
    count = 8
    first = rotor_blocks[:, 0]
    line = first // x_blocks
    zs = line // NY - lax.axis_index("wide") * shard_z
    ys = line % NY - lax.axis_index("narrow") * shard_y
    xs = first % x_blocks
    field = lambda c: pl.BlockSpec((None, shard_z, shard_y, extent), lambda i, *_: (c, 0, 0, 0))
    sums = pl.BlockSpec((count, 128), lambda i, *_: (i, 0))
    return pl.pallas_call(
        functools.partial(turbine_kernel, count, (shard_z, shard_y, blocks // RY)),
        grid_spec=pltpu.PrefetchScalarGridSpec(
            num_scalar_prefetch=4,
            grid=(turbines // count,),
            in_specs=[
                field(0),
                field(1),
                field(0),
                pl.BlockSpec((count, blocks, 128), lambda i, *_: (i, 0, 0)),
            ],
            out_specs=[
                pl.BlockSpec((shard_z, shard_y, extent), lambda i, *_: (0, 0, 0)),
                sums,
                sums,
            ],
        ),
        out_shape=[
            jax.ShapeDtypeStruct((shard_z, shard_y, extent), jnp.float32),
            jax.ShapeDtypeStruct((turbines, 128), jnp.float32),
            jax.ShapeDtypeStruct((turbines, 128), jnp.float32),
        ],
        compiler_params=params(),
        cost_estimate=cost(1e6, 3e7),
        name="turbine_terms",
    )(zs, ys, xs, thrust, adjoint, adjoint, velocity, disk_weight)


def z_local_kernel(matrix, adjoint, velocity, out):
    _, shard_z, group, extent = adjoint.shape
    rows = shard_z * group
    both = matrix[...]
    high_part = both[:rows]

    def derivative(values):
        high, low = split(values.reshape(rows, extent))
        wide = dot(both, high)
        total = wide[:rows] + wide[rows:] + dot(high_part, low)
        return total.reshape(shard_z, group, extent)

    carrier = velocity[2]
    stretch = adjoint[0] * derivative(velocity[0])
    stretch += adjoint[1] * derivative(velocity[1])
    stretch += adjoint[2] * derivative(velocity[2])
    out[0] = carrier * derivative(adjoint[0])
    out[1] = carrier * derivative(adjoint[1])
    out[2] = carrier * derivative(adjoint[2]) - stretch


def z_local(matrix, adjoint, velocity):
    _, shard_z, shard_y, extent = adjoint.shape
    block = pl.BlockSpec((3, shard_z, GROUP, extent), lambda i: (0, 0, i, 0))
    return pl.pallas_call(
        z_local_kernel,
        grid=(shard_y // GROUP,),
        in_specs=[pl.BlockSpec(matrix.shape, lambda i: (0, 0)), block, block],
        out_specs=block,
        out_shape=jax.ShapeDtypeStruct(adjoint.shape, jnp.float32),
        compiler_params=params(),
        cost_estimate=cost(2e10, 4e7),
        name="z_local",
    )(matrix, adjoint, velocity)


def xy_kernel(
    matrix_x, matrix_ya, matrix_yv, edge_low, edge_high,
    adjoint, velocity, halo_low, halo_high, source, tendency, out, back_low, back_high,
):
    _, planes, shard_y, extent = adjoint.shape
    rows = planes * shard_y
    x_high = matrix_x[:, :extent]
    x_low = matrix_x[:, extent:]

    def along_x(values):
        high, low = split(values.reshape(rows, extent))
        total = dot(high, x_high) + (dot(low, x_high) + dot(high, x_low))
        return total.reshape(planes, shard_y, extent)

    a0, a1, a2 = adjoint[0], adjoint[1], adjoint[2]
    u = velocity[0]
    stretch = a0 * along_x(velocity[0])
    stretch += a1 * along_x(velocity[1])
    stretch += a2 * along_x(velocity[2])
    out[0] = tendency[0] + u * along_x(a0) - stretch - source[...] * jnp.abs(u) * a0
    out[1] = tendency[1] + u * along_x(a1)
    out[2] = tendency[2] + u * along_x(a2)
    for plane in range(planes):
        stretch = jnp.zeros((shard_y, extent), jnp.float32)
        low_sum = jnp.zeros((BY, extent), jnp.float32)
        high_sum = jnp.zeros((BY, extent), jnp.float32)
        carrier = velocity[1, plane]
        for c in range(3):
            value = velocity[c, plane]
            here = adjoint[c, plane]
            below = halo_low[c, plane]
            above = halo_high[c, plane]
            stretch += here * apply_stacked(matrix_yv[...], value)
            low_sum += below * apply_stacked(edge_low[...], value[:BY])
            high_sum += above * apply_stacked(edge_high[...], value[shard_y - BY :])
            column = jnp.concatenate([below, here, above], axis=0)
            out[c, plane] += carrier * apply_stacked(matrix_ya[...], column)
        out[1, plane] -= stretch
        back_low[plane] = low_sum
        back_high[plane] = high_sum


def xy_terms(matrices, adjoint, velocity, halo_low, halo_high, source, tendency):
    _, shard_z, shard_y, extent = adjoint.shape
    planes = 4
    whole = lambda m: pl.BlockSpec(m.shape, lambda i: (0, 0))
    block = pl.BlockSpec((3, planes, shard_y, extent), lambda i: (0, i, 0, 0))
    halo = pl.BlockSpec((3, planes, BY, extent), lambda i: (0, i, 0, 0))
    back = pl.BlockSpec((planes, BY, extent), lambda i: (i, 0, 0))
    plane = pl.BlockSpec((planes, shard_y, extent), lambda i: (i, 0, 0))
    back_shape = jax.ShapeDtypeStruct((shard_z, BY, extent), jnp.float32)
    return pl.pallas_call(
        xy_kernel,
        grid=(shard_z // planes,),
        in_specs=[whole(m) for m in matrices] + [block, block, halo, halo, plane, block],
        out_specs=[block, back, back],
        out_shape=[jax.ShapeDtypeStruct(adjoint.shape, jnp.float32), back_shape, back_shape],
        compiler_params=params(),
        cost_estimate=cost(2e10, 7e7),
        name="xy_terms",
    )(*matrices, adjoint, velocity, halo_low, halo_high, source, tendency)


def z_back_kernel(edge_low, edge_high, vel_low, vel_high, halo_low, halo_high, back_low, back_high):
    _, band, group, extent = vel_low.shape
    rows = band * group
    for edge, vel, halo, back in (
        (edge_low, vel_low, halo_low, back_low),
        (edge_high, vel_high, halo_high, back_high),
    ):
        total = jnp.zeros((rows, extent), jnp.float32)
        for c in range(3):
            value = vel[c].reshape(rows, extent)
            total += halo[c].reshape(rows, extent) * apply_stacked(edge[...], value)
        back[...] = total.reshape(band, group, extent)


def z_back(edge_low, edge_high, velocity, halo_low, halo_high):
    _, shard_z, shard_y, extent = velocity.shape
    last = shard_z // BAND - 1
    whole = lambda m: pl.BlockSpec(m.shape, lambda i: (0, 0))
    edge = lambda at: pl.BlockSpec((3, BAND, GROUP, extent), lambda i: (0, at, i, 0))
    back = pl.BlockSpec((BAND, GROUP, extent), lambda i: (0, i, 0))
    shape = jax.ShapeDtypeStruct((BAND, shard_y, extent), jnp.float32)
    return pl.pallas_call(
        z_back_kernel,
        grid=(shard_y // GROUP,),
        in_specs=[whole(edge_low), whole(edge_high), edge(0), edge(last), edge(0), edge(0)],
        out_specs=[back, back],
        out_shape=[shape, shape],
        compiler_params=params(),
        cost_estimate=cost(3e9, 2e7),
        name="z_back",
    )(edge_low, edge_high, velocity, velocity, halo_low, halo_high)


def combine_kernel(
    from_low, from_high, adjoint, carrier, tendency, halo_low, halo_high, stretch_y, out
):
    _, shard_z, group, extent = adjoint.shape
    rows = BAND * group
    top = shard_z - BAND
    for c in range(3):
        total = tendency[c]
        if c == 1:
            total = total - stretch_y[...]
        out[c] = adjoint[c] + STEP * total
        for matrix, halo, at in ((from_low, halo_low, 0), (from_high, halo_high, top)):
            part = apply_stacked(matrix[...], halo[c].reshape(rows, extent))
            planes = slice(at, at + BAND)
            out[c, planes] += STEP * (carrier[planes] * part.reshape(BAND, group, extent))


def combine(from_low, from_high, adjoint, velocity, tendency, halo_low, halo_high, stretch_y):
    _, shard_z, shard_y, extent = adjoint.shape
    whole = lambda m: pl.BlockSpec(m.shape, lambda i: (0, 0))
    block = pl.BlockSpec((3, shard_z, GROUP, extent), lambda i: (0, 0, i, 0))
    carrier = pl.BlockSpec((None, shard_z, GROUP, extent), lambda i: (2, 0, i, 0))
    halo = pl.BlockSpec((3, BAND, GROUP, extent), lambda i: (0, 0, i, 0))
    plane = pl.BlockSpec((shard_z, GROUP, extent), lambda i: (0, i, 0))
    return pl.pallas_call(
        combine_kernel,
        grid=(shard_y // GROUP,),
        in_specs=[whole(from_low), whole(from_high), block, carrier, block, halo, halo, plane],
        out_specs=block,
        out_shape=jax.ShapeDtypeStruct(adjoint.shape, jnp.float32),
        compiler_params=params(),
        cost_estimate=cost(3e9, 5e7),
        name="combine",
    )(from_low, from_high, adjoint, velocity, tendency, halo_low, halo_high, stretch_y)


def finish_kernel(back_low, back_high, updated, out):
    back = jnp.where(pl.program_id(0) == 0, back_low[...], back_high[...])
    out[...] = updated[...] - STEP * back


def finish(updated, back_low, back_high):
    _, shard_z, shard_y, extent = updated.shape
    last = shard_z // BAND - 1
    lines = 16
    edge = pl.BlockSpec((None, BAND, lines, extent), lambda i, j: (2, i * last, j, 0))
    back = pl.BlockSpec((BAND, lines, extent), lambda i, j: (0, j, 0))
    return pl.pallas_call(
        finish_kernel,
        grid=(2, shard_y // lines),
        in_specs=[back, back, edge],
        out_specs=edge,
        out_shape=jax.ShapeDtypeStruct(updated.shape, jnp.float32),
        input_output_aliases={2: 0},
        compiler_params=params(),
        cost_estimate=cost(1e6, 6e6),
        name="finish",
    )(back_low, back_high, updated)


def send_up(value, axis):
    size = lax.axis_size(axis)
    return lax.ppermute(value, axis, [(i, i + 1) for i in range(size - 1)])


def send_down(value, axis):
    size = lax.axis_size(axis)
    return lax.ppermute(value, axis, [(i + 1, i) for i in range(size - 1)])


def windows(matrix, first, shard, halo):
    padded = jnp.pad(matrix, halo)
    rows = lax.dynamic_slice(padded, (first + halo, first), (shard, shard + 2 * halo))
    to_low = lax.dynamic_slice(padded, (first, first + halo), (halo, halo))
    to_high = lax.dynamic_slice(padded, (first + shard + halo, first + shard), (halo, halo))
    return rows, to_low, to_high


def owner_rows(partial_value, turbine_owner):
    turbines = turbine_owner.shape[0]
    devices = lax.axis_size("wide") * lax.axis_size("narrow")
    slot_count = (turbines - 2) // devices + 2
    device = lax.axis_index("wide") * lax.axis_size("narrow") + lax.axis_index("narrow")
    gathered = lax.all_gather(partial_value, ("wide", "narrow"), axis=0, tiled=False)
    grad = jnp.sum(gathered, axis=0)
    positions = jnp.arange(turbines)
    shared = turbine_owner[:, None] == turbine_owner[None, :]
    earlier = positions[:, None] > positions[None, :]
    slot_rank = jnp.sum((shared & earlier).astype(jnp.int32), axis=1)
    mine = (turbine_owner[None, :] == device) & (jnp.arange(slot_count)[:, None] == slot_rank[None, :])
    return jnp.sum(jnp.where(mine[:, None, :], grad[None], 0.0), axis=2)


def on_device(
    adjoint, velocity, deriv_x, deriv_y, deriv_z, rotor_blocks, turbine_owner, disk_weight, thrust
):
    _, shard_z, shard_y, extent = adjoint.shape
    z_low = send_up(adjoint[:, shard_z - BAND :], "wide")
    z_high = send_down(adjoint[:, :BAND], "wide")
    y_low = send_up(adjoint[:, :, shard_y - BY :], "narrow")
    y_high = send_down(adjoint[:, :, :BY], "narrow")

    rows_z, z_to_low, z_to_high = windows(
        deriv_z, lax.axis_index("wide") * shard_z, shard_z, BAND
    )
    rows_y, y_to_low, y_to_high = windows(
        deriv_y, lax.axis_index("narrow") * shard_y, shard_y, BY
    )
    lanes = jnp.eye(GROUP, dtype=jnp.float32)
    spread = lambda m: jnp.kron(m, lanes)

    source, grad0, grad1 = turbine_terms(adjoint, velocity, rotor_blocks, disk_weight, thrust)
    scale = 1.0 / math.sqrt(128.0 * rotor_blocks.shape[1])
    partial_value = jnp.stack([jnp.sum(grad0, axis=1), jnp.sum(grad1, axis=1)]) * scale
    turbine_grad = owner_rows(partial_value, turbine_owner)

    local_z = paired(spread(rows_z[:, BAND : BAND + shard_z]), 0)
    tendency = z_local(local_z, adjoint, velocity)
    matrices = (
        paired(deriv_x.T, 1),
        stacked(rows_y),
        stacked(rows_y[:, BY : BY + shard_y]),
        stacked(y_to_low),
        stacked(y_to_high),
    )
    tendency, y_back_low, y_back_high = xy_terms(
        matrices, adjoint, velocity, y_low, y_high, source, tendency
    )
    stretch_low = send_up(y_back_high, "narrow")
    stretch_high = send_down(y_back_low, "narrow")
    rest = shard_y - BY
    stretch_y = jnp.pad(stretch_low, ((0, 0), (0, rest), (0, 0))) + jnp.pad(
        stretch_high, ((0, 0), (rest, 0), (0, 0))
    )
    z_back_low, z_back_high = z_back(
        stacked(spread(z_to_low)), stacked(spread(z_to_high)), velocity, z_low, z_high
    )
    last_low = send_up(z_back_high, "wide")
    last_high = send_down(z_back_low, "wide")
    updated = combine(
        stacked(spread(rows_z[:BAND, :BAND])),
        stacked(spread(rows_z[shard_z - BAND :, BAND + shard_z :])),
        adjoint, velocity, tendency, z_low, z_high, stretch_y,
    )
    return finish(updated, last_low, last_high), turbine_grad


def solution(mesh):
    return jax.shard_map(
        on_device,
        mesh=mesh,
        in_specs=(
            P(None, "wide", "narrow", None),
            P(None, "wide", "narrow", None),
            P(),
            P(),
            P(),
            P(),
            P(),
            P(),
            P(),
        ),
        out_specs=(P(None, "wide", "narrow", None), P(("wide", "narrow"), None)),
        check_vma=False,
    )
```

```python
import functools
import math

import jax
import jax.numpy as jnp
from jax import lax
from jax.experimental import pallas as pl
from jax.experimental.pallas import tpu as pltpu
from jax.sharding import PartitionSpec as P

NY = 256
BY = 32
BAND = 16
RY = 2
STEP = 0.2
GROUP = 8
VMEM = 56 * 1024 * 1024


def params(limit=VMEM):
    return pltpu.CompilerParams(vmem_limit_bytes=limit)


def cost(flops, moved):
    return pl.CostEstimate(flops=int(flops / 50), bytes_accessed=int(moved / 50), transcendentals=0)


def split(value):
    high = value.astype(jnp.bfloat16)
    low = (value - high.astype(jnp.float32)).astype(jnp.bfloat16)
    return high, low


def dot(left, right):
    return jnp.dot(left, right, preferred_element_type=jnp.float32)


def picked(window, rows, first_row, columns, first_column, repeat, copies):
    size = window.shape[0]
    height, width = rows * repeat, columns * repeat * copies
    i = lax.broadcasted_iota(jnp.int32, (height, size), 0)
    k = lax.broadcasted_iota(jnp.int32, (height, size), 1)
    left = (lax.div(i, repeat) + first_row == k).astype(jnp.float32).astype(jnp.bfloat16)
    k = lax.broadcasted_iota(jnp.int32, (size, width), 0)
    j = lax.rem(lax.broadcasted_iota(jnp.int32, (size, width), 1), columns * repeat)
    right = (lax.div(j, repeat) + first_column == k).astype(jnp.float32).astype(jnp.bfloat16)
    block = dot(dot(left, window).astype(jnp.bfloat16), right)
    i = lax.broadcasted_iota(jnp.int32, (height, width), 0)
    j = lax.broadcasted_iota(jnp.int32, (height, width), 1)
    return jnp.where(lax.rem(i, repeat) == lax.rem(j, repeat), block, 0.0), j


def stacked(window, rows, first_row, columns, first_column, repeat):
    high, low = window
    top, j = picked(high, rows, first_row, columns, first_column, repeat, 2)
    bottom, _ = picked(low, rows, first_row, columns, first_column, repeat, 2)
    bottom = jnp.where(j < columns * repeat, bottom, 0.0)
    return jnp.concatenate([top, bottom], axis=0).astype(jnp.bfloat16)


def matrices_kernel(
    shard_z, shard_y, x, y, z,
    x_pair, y_full, y_local, y_to_low, y_to_high,
    z_pair, z_from_low, z_from_high, z_to_low, z_to_high,
):
    high, low = split(x[...].T)
    x_pair[:, : high.shape[1]] = high
    x_pair[:, high.shape[1] :] = low
    window = split(y[...])
    y_full[...] = stacked(window, shard_y, BY, shard_y + 2 * BY, 0, 1)
    y_local[...] = stacked(window, shard_y, BY, shard_y, BY, 1)
    y_to_low[...] = stacked(window, BY, 0, BY, BY, 1)
    y_to_high[...] = stacked(window, BY, shard_y + BY, BY, shard_y, 1)
    window = split(z[...])
    rows = shard_z * GROUP
    for at in range(2):
        block, _ = picked(window[at], shard_z, BAND, shard_z, BAND, GROUP, 1)
        z_pair[at * rows : (at + 1) * rows, :] = block.astype(jnp.bfloat16)
    z_from_low[...] = stacked(window, BAND, BAND, BAND, 0, GROUP)
    z_from_high[...] = stacked(window, BAND, shard_z, BAND, shard_z + BAND, GROUP)
    z_to_low[...] = stacked(window, BAND, 0, BAND, BAND, GROUP)
    z_to_high[...] = stacked(window, BAND, shard_z + BAND, BAND, shard_z, GROUP)


def window(matrix, first, shard, halo):
    return lax.dynamic_slice(jnp.pad(matrix, halo), (first, first), (shard + 2 * halo,) * 2)


def matrices(deriv_x, deriv_y, deriv_z, shard_z, shard_y):
    extent = deriv_x.shape[0]
    z = window(deriv_z, lax.axis_index("wide") * shard_z, shard_z, BAND)
    y = window(deriv_y, lax.axis_index("narrow") * shard_y, shard_y, BY)
    edge = 2 * BAND * GROUP
    rows = shard_z * GROUP
    shapes = [
        (extent, 2 * extent),
        (2 * shard_y, 2 * (shard_y + 2 * BY)),
        (2 * shard_y, 2 * shard_y),
        (2 * BY, 2 * BY),
        (2 * BY, 2 * BY),
        (2 * rows, rows),
    ] + [(edge, edge)] * 4
    out = pl.pallas_call(
        functools.partial(matrices_kernel, shard_z, shard_y),
        out_shape=[jax.ShapeDtypeStruct(shape, jnp.bfloat16) for shape in shapes],
        compiler_params=params(24 * 1024 * 1024),
        cost_estimate=cost(1e8, 4e6),
        name="matrices",
    )(deriv_x, y, z)
    return out[:5], out[5], out[6:8], out[8:10]


def apply_stacked(matrix, values):
    product = dot(matrix, jnp.concatenate(split(values), axis=0))
    rows = product.shape[0] // 2
    return product[:rows] + product[rows:]


def turbine_kernel(
    count, shard, zs, ys, xs, thrust, a0, a1, u0, weight, source, grad0, grad1
):
    shard_z, shard_y, planes = shard
    step = pl.program_id(0)

    @pl.when(step == 0)
    def _():
        source[...] = jnp.zeros_like(source)

    grad0[...] = jnp.zeros_like(grad0)
    grad1[...] = jnp.zeros_like(grad1)
    for slot in range(count):
        turbine = step * count + slot
        first_z = zs[turbine]
        low = jnp.maximum(first_z, 0)
        high = jnp.minimum(first_z + planes, shard_z)
        lanes = pl.ds(pl.multiple_of(xs[turbine] * 128, 128), 128)
        for line in range(RY):
            y = ys[turbine] + line

            @pl.when((y >= 0) & (y < shard_y) & (high > low))
            def _():
                tile = pl.ds(pl.multiple_of(y // 8 * 8, 8), 8)
                chosen = lax.broadcasted_iota(jnp.int32, (8, 128), 0) == y % 8

                def body(z, sums):
                    row = weight[slot, pl.ds((z - first_z) * RY + line, 1), :]
                    row = jnp.where(chosen, jnp.broadcast_to(row, (8, 128)), 0.0)
                    at = (z, tile, lanes)
                    u = u0[at]
                    driven = row * u * jnp.abs(u)
                    source[at] += row * thrust[turbine]
                    return sums[0] + driven * a0[at], sums[1] + driven * a1[at]

                zero = jnp.zeros((8, 128), jnp.float32)
                sums = lax.fori_loop(low, high, body, (zero, zero))
                grad0[slot : slot + 1, :] += jnp.sum(sums[0], axis=0, keepdims=True)
                grad1[slot : slot + 1, :] += jnp.sum(sums[1], axis=0, keepdims=True)


def turbine_terms(adjoint, velocity, rotor_blocks, disk_weight, thrust):
    _, shard_z, shard_y, extent = adjoint.shape
    x_blocks = extent // 128
    turbines, blocks = rotor_blocks.shape
    count = 8
    first = rotor_blocks[:, 0]
    line = first // x_blocks
    zs = line // NY - lax.axis_index("wide") * shard_z
    ys = line % NY - lax.axis_index("narrow") * shard_y
    xs = first % x_blocks
    field = lambda c: pl.BlockSpec((None, shard_z, shard_y, extent), lambda i, *_: (c, 0, 0, 0))
    sums = pl.BlockSpec((count, 128), lambda i, *_: (i, 0))
    return pl.pallas_call(
        functools.partial(turbine_kernel, count, (shard_z, shard_y, blocks // RY)),
        grid_spec=pltpu.PrefetchScalarGridSpec(
            num_scalar_prefetch=4,
            grid=(turbines // count,),
            in_specs=[
                field(0),
                field(1),
                field(0),
                pl.BlockSpec((count, blocks, 128), lambda i, *_: (i, 0, 0)),
            ],
            out_specs=[
                pl.BlockSpec((shard_z, shard_y, extent), lambda i, *_: (0, 0, 0)),
                sums,
                sums,
            ],
        ),
        out_shape=[
            jax.ShapeDtypeStruct((shard_z, shard_y, extent), jnp.float32),
            jax.ShapeDtypeStruct((turbines, 128), jnp.float32),
            jax.ShapeDtypeStruct((turbines, 128), jnp.float32),
        ],
        compiler_params=params(),
        cost_estimate=cost(1e6, 3e7),
        name="turbine_terms",
    )(zs, ys, xs, thrust, adjoint, adjoint, velocity, disk_weight)


def z_local_kernel(matrix, adjoint, velocity, out):
    _, shard_z, group, extent = adjoint.shape
    rows = shard_z * group
    both = matrix[...]
    high_part = both[:rows]

    def derivative(values):
        high, low = split(values.reshape(rows, extent))
        wide = dot(both, high)
        total = wide[:rows] + wide[rows:] + dot(high_part, low)
        return total.reshape(shard_z, group, extent)

    carrier = velocity[2]
    stretch = adjoint[0] * derivative(velocity[0])
    stretch += adjoint[1] * derivative(velocity[1])
    stretch += adjoint[2] * derivative(velocity[2])
    out[0] = carrier * derivative(adjoint[0])
    out[1] = carrier * derivative(adjoint[1])
    out[2] = carrier * derivative(adjoint[2]) - stretch


def z_local(matrix, adjoint, velocity):
    _, shard_z, shard_y, extent = adjoint.shape
    block = pl.BlockSpec((3, shard_z, GROUP, extent), lambda i: (0, 0, i, 0))
    return pl.pallas_call(
        z_local_kernel,
        grid=(shard_y // GROUP,),
        in_specs=[pl.BlockSpec(matrix.shape, lambda i: (0, 0)), block, block],
        out_specs=block,
        out_shape=jax.ShapeDtypeStruct(adjoint.shape, jnp.float32),
        compiler_params=params(),
        cost_estimate=cost(2e10, 4e7),
        name="z_local",
    )(matrix, adjoint, velocity)


def xy_kernel(
    matrix_x, matrix_ya, matrix_yv, edge_low, edge_high,
    adjoint, velocity, halo_low, halo_high, source, tendency, out, back_low, back_high,
):
    _, planes, shard_y, extent = adjoint.shape
    rows = planes * shard_y
    x_high = matrix_x[:, :extent]
    x_low = matrix_x[:, extent:]

    def along_x(values):
        high, low = split(values.reshape(rows, extent))
        total = dot(high, x_high) + (dot(low, x_high) + dot(high, x_low))
        return total.reshape(planes, shard_y, extent)

    a0, a1, a2 = adjoint[0], adjoint[1], adjoint[2]
    u = velocity[0]
    stretch = a0 * along_x(velocity[0])
    stretch += a1 * along_x(velocity[1])
    stretch += a2 * along_x(velocity[2])
    out[0] = tendency[0] + u * along_x(a0) - stretch - source[...] * jnp.abs(u) * a0
    out[1] = tendency[1] + u * along_x(a1)
    out[2] = tendency[2] + u * along_x(a2)
    for plane in range(planes):
        stretch = jnp.zeros((shard_y, extent), jnp.float32)
        low_sum = jnp.zeros((BY, extent), jnp.float32)
        high_sum = jnp.zeros((BY, extent), jnp.float32)
        carrier = velocity[1, plane]
        for c in range(3):
            value = velocity[c, plane]
            here = adjoint[c, plane]
            below = halo_low[c, plane]
            above = halo_high[c, plane]
            stretch += here * apply_stacked(matrix_yv[...], value)
            low_sum += below * apply_stacked(edge_low[...], value[:BY])
            high_sum += above * apply_stacked(edge_high[...], value[shard_y - BY :])
            column = jnp.concatenate([below, here, above], axis=0)
            out[c, plane] += carrier * apply_stacked(matrix_ya[...], column)
        out[1, plane] -= stretch
        back_low[plane] = low_sum
        back_high[plane] = high_sum


def xy_terms(operators, adjoint, velocity, halo_low, halo_high, source, tendency):
    _, shard_z, shard_y, extent = adjoint.shape
    planes = 4
    whole = lambda m: pl.BlockSpec(m.shape, lambda i: (0, 0))
    block = pl.BlockSpec((3, planes, shard_y, extent), lambda i: (0, i, 0, 0))
    halo = pl.BlockSpec((3, planes, BY, extent), lambda i: (0, i, 0, 0))
    back = pl.BlockSpec((planes, BY, extent), lambda i: (i, 0, 0))
    plane = pl.BlockSpec((planes, shard_y, extent), lambda i: (i, 0, 0))
    back_shape = jax.ShapeDtypeStruct((shard_z, BY, extent), jnp.float32)
    return pl.pallas_call(
        xy_kernel,
        grid=(shard_z // planes,),
        in_specs=[whole(m) for m in operators] + [block, block, halo, halo, plane, block],
        out_specs=[block, back, back],
        out_shape=[jax.ShapeDtypeStruct(adjoint.shape, jnp.float32), back_shape, back_shape],
        compiler_params=params(),
        cost_estimate=cost(2e10, 7e7),
        name="xy_terms",
    )(*operators, adjoint, velocity, halo_low, halo_high, source, tendency)


def z_back_kernel(edge_low, edge_high, vel_low, vel_high, halo_low, halo_high, back_low, back_high):
    _, band, group, extent = vel_low.shape
    rows = band * group
    for edge, vel, halo, back in (
        (edge_low, vel_low, halo_low, back_low),
        (edge_high, vel_high, halo_high, back_high),
    ):
        total = jnp.zeros((rows, extent), jnp.float32)
        for c in range(3):
            value = vel[c].reshape(rows, extent)
            total += halo[c].reshape(rows, extent) * apply_stacked(edge[...], value)
        back[...] = total.reshape(band, group, extent)


def z_back(edge_low, edge_high, velocity, halo_low, halo_high):
    _, shard_z, shard_y, extent = velocity.shape
    last = shard_z // BAND - 1
    whole = lambda m: pl.BlockSpec(m.shape, lambda i: (0, 0))
    edge = lambda at: pl.BlockSpec((3, BAND, GROUP, extent), lambda i: (0, at, i, 0))
    back = pl.BlockSpec((BAND, GROUP, extent), lambda i: (0, i, 0))
    shape = jax.ShapeDtypeStruct((BAND, shard_y, extent), jnp.float32)
    return pl.pallas_call(
        z_back_kernel,
        grid=(shard_y // GROUP,),
        in_specs=[whole(edge_low), whole(edge_high), edge(0), edge(last), edge(0), edge(0)],
        out_specs=[back, back],
        out_shape=[shape, shape],
        compiler_params=params(16 * 1024 * 1024),
        cost_estimate=cost(3e9, 2e7),
        name="z_back",
    )(edge_low, edge_high, velocity, velocity, halo_low, halo_high)


def combine_kernel(
    from_low, from_high, adjoint, carrier, tendency, halo_low, halo_high, stretch_y, out
):
    _, shard_z, group, extent = adjoint.shape
    rows = BAND * group
    top = shard_z - BAND
    for c in range(3):
        total = tendency[c]
        if c == 1:
            total = total - stretch_y[...]
        out[c] = adjoint[c] + STEP * total
        for matrix, halo, at in ((from_low, halo_low, 0), (from_high, halo_high, top)):
            part = apply_stacked(matrix[...], halo[c].reshape(rows, extent))
            planes = slice(at, at + BAND)
            out[c, planes] += STEP * (carrier[planes] * part.reshape(BAND, group, extent))


def combine(from_low, from_high, adjoint, velocity, tendency, halo_low, halo_high, stretch_y):
    _, shard_z, shard_y, extent = adjoint.shape
    whole = lambda m: pl.BlockSpec(m.shape, lambda i: (0, 0))
    block = pl.BlockSpec((3, shard_z, GROUP, extent), lambda i: (0, 0, i, 0))
    carrier = pl.BlockSpec((None, shard_z, GROUP, extent), lambda i: (2, 0, i, 0))
    halo = pl.BlockSpec((3, BAND, GROUP, extent), lambda i: (0, 0, i, 0))
    plane = pl.BlockSpec((shard_z, GROUP, extent), lambda i: (0, i, 0))
    return pl.pallas_call(
        combine_kernel,
        grid=(shard_y // GROUP,),
        in_specs=[whole(from_low), whole(from_high), block, carrier, block, halo, halo, plane],
        out_specs=block,
        out_shape=jax.ShapeDtypeStruct(adjoint.shape, jnp.float32),
        compiler_params=params(),
        cost_estimate=cost(3e9, 5e7),
        name="combine",
    )(from_low, from_high, adjoint, velocity, tendency, halo_low, halo_high, stretch_y)


def finish_kernel(back_low, back_high, updated, out):
    back = jnp.where(pl.program_id(0) == 0, back_low[...], back_high[...])
    out[...] = updated[...] - STEP * back


def finish(updated, back_low, back_high):
    _, shard_z, shard_y, extent = updated.shape
    last = shard_z // BAND - 1
    lines = 16
    edge = pl.BlockSpec((None, BAND, lines, extent), lambda i, j: (2, i * last, j, 0))
    back = pl.BlockSpec((BAND, lines, extent), lambda i, j: (0, j, 0))
    return pl.pallas_call(
        finish_kernel,
        grid=(2, shard_y // lines),
        in_specs=[back, back, edge],
        out_specs=edge,
        out_shape=jax.ShapeDtypeStruct(updated.shape, jnp.float32),
        input_output_aliases={2: 0},
        compiler_params=params(8 * 1024 * 1024),
        cost_estimate=cost(1e6, 6e6),
        name="finish",
    )(back_low, back_high, updated)


def send_up(value, axis):
    size = lax.axis_size(axis)
    return lax.ppermute(value, axis, [(i, i + 1) for i in range(size - 1)])


def send_down(value, axis):
    size = lax.axis_size(axis)
    return lax.ppermute(value, axis, [(i + 1, i) for i in range(size - 1)])


def exchange(value, axis, distance):
    size = lax.axis_size(axis)
    return lax.ppermute(value, axis, [(i, i ^ distance) for i in range(size)])


def after(value, *others):
    return lax.optimization_barrier((value, *others))


def owner_rows(grad, turbine_owner):
    turbines = turbine_owner.shape[0]
    devices = lax.axis_size("wide") * lax.axis_size("narrow")
    slot_count = (turbines - 2) // devices + 2
    device = lax.axis_index("wide") * lax.axis_size("narrow") + lax.axis_index("narrow")
    positions = jnp.arange(turbines)
    shared = turbine_owner[:, None] == turbine_owner[None, :]
    earlier = positions[:, None] > positions[None, :]
    slot_rank = jnp.sum((shared & earlier).astype(jnp.int32), axis=1)
    mine = (turbine_owner[None, :] == device) & (jnp.arange(slot_count)[:, None] == slot_rank[None, :])
    return jnp.sum(jnp.where(mine[:, None, :], grad[None], 0.0), axis=2)


def on_device(
    adjoint, velocity, deriv_x, deriv_y, deriv_z, rotor_blocks, turbine_owner, disk_weight, thrust
):
    _, shard_z, shard_y, extent = adjoint.shape
    z_low = send_up(adjoint[:, shard_z - BAND :], "wide")
    z_high = send_down(adjoint[:, :BAND], "wide")
    xy_matrices, z_pair, z_from, z_to = matrices(deriv_x, deriv_y, deriv_z, shard_z, shard_y)
    z_pair, adjoint = after(z_pair, adjoint)
    y_low = send_up(adjoint[:, :, shard_y - BY :], "narrow")
    y_high = send_down(adjoint[:, :, :BY], "narrow")

    steps = [("narrow", 2**k) for k in range(8) if 2**k < lax.axis_size("narrow")]
    steps += [("wide", 2**k) for k in range(8) if 2**k < lax.axis_size("wide")]

    source, grad0, grad1 = turbine_terms(adjoint, velocity, rotor_blocks, disk_weight, thrust)
    scale = 1.0 / math.sqrt(128.0 * rotor_blocks.shape[1])
    grad = jnp.stack([jnp.sum(grad0, axis=1), jnp.sum(grad1, axis=1)]) * scale

    moved = exchange(grad, *steps[0])
    tendency = z_local(z_pair, adjoint, velocity)
    moved, tendency = after(moved, tendency)
    grad = grad + moved
    moved = exchange(grad, *steps[1])
    moved, y_low, y_high = after(moved, y_low, y_high)
    grad = grad + moved
    moved = exchange(grad, *steps[2])
    tendency, y_back_low, y_back_high = xy_terms(
        xy_matrices, adjoint, velocity, y_low, y_high, source, tendency
    )
    moved, y_back_low, y_back_high = after(moved, y_back_low, y_back_high)
    grad = grad + moved
    stretch_low = send_up(y_back_high, "narrow")
    stretch_high = send_down(y_back_low, "narrow")
    moved = exchange(grad, *steps[3])
    moved, z_low, z_high = after(moved, z_low, z_high)
    grad = grad + moved
    z_back_low, z_back_high = z_back(*z_to, velocity, z_low, z_high)
    last_low = send_up(z_back_high, "wide")
    last_high = send_down(z_back_low, "wide")
    rest = shard_y - BY
    stretch_y = jnp.pad(stretch_low, ((0, 0), (0, rest), (0, 0))) + jnp.pad(
        stretch_high, ((0, 0), (rest, 0), (0, 0))
    )
    moved = exchange(grad, *steps[4])
    updated = combine(*z_from, adjoint, velocity, tendency, z_low, z_high, stretch_y)
    moved, updated = after(moved, updated)
    grad = grad + moved
    for step in steps[5:]:
        grad = grad + exchange(grad, *step)
    return finish(updated, last_low, last_high), owner_rows(grad, turbine_owner)


def solution(mesh):
    return jax.shard_map(
        on_device,
        mesh=mesh,
        in_specs=(
            P(None, "wide", "narrow", None),
            P(None, "wide", "narrow", None),
            P(),
            P(),
            P(),
            P(),
            P(),
            P(),
            P(),
        ),
        out_specs=(P(None, "wide", "narrow", None), P(("wide", "narrow"), None)),
        check_vma=False,
    )
```

```python
import functools
import math

import jax
import jax.numpy as jnp
from jax import lax
from jax.experimental import pallas as pl
from jax.experimental.pallas import tpu as pltpu
from jax.sharding import PartitionSpec as P

NY = 256
BY = 32
BAND = 16
RY = 2
STEP = 0.2
GROUP = 8
VMEM = 56 * 1024 * 1024


def params(limit=VMEM):
    return pltpu.CompilerParams(vmem_limit_bytes=limit)


def cost(flops, moved):
    return pl.CostEstimate(flops=int(flops / 50), bytes_accessed=int(moved / 50), transcendentals=0)


def split(value):
    high = value.astype(jnp.bfloat16)
    low = (value - high.astype(jnp.float32)).astype(jnp.bfloat16)
    return high, low


def dot(left, right):
    return jnp.dot(left, right, preferred_element_type=jnp.float32)


def picked(window, rows, first_row, columns, first_column, repeat, copies):
    size = window.shape[0]
    height, width = rows * repeat, columns * repeat * copies
    i = lax.broadcasted_iota(jnp.int32, (height, size), 0)
    k = lax.broadcasted_iota(jnp.int32, (height, size), 1)
    left = (lax.div(i, repeat) + first_row == k).astype(jnp.float32).astype(jnp.bfloat16)
    k = lax.broadcasted_iota(jnp.int32, (size, width), 0)
    j = lax.rem(lax.broadcasted_iota(jnp.int32, (size, width), 1), columns * repeat)
    right = (lax.div(j, repeat) + first_column == k).astype(jnp.float32).astype(jnp.bfloat16)
    block = dot(dot(left, window).astype(jnp.bfloat16), right)
    i = lax.broadcasted_iota(jnp.int32, (height, width), 0)
    j = lax.broadcasted_iota(jnp.int32, (height, width), 1)
    return jnp.where(lax.rem(i, repeat) == lax.rem(j, repeat), block, 0.0), j


def stacked(window, rows, first_row, columns, first_column, repeat):
    high, low = window
    top, j = picked(high, rows, first_row, columns, first_column, repeat, 2)
    bottom, _ = picked(low, rows, first_row, columns, first_column, repeat, 2)
    bottom = jnp.where(j < columns * repeat, bottom, 0.0)
    return jnp.concatenate([top, bottom], axis=0).astype(jnp.bfloat16)


def matrices_kernel(
    shard_z, shard_y, x, y, z,
    x_pair, y_full, y_local, y_to_low, y_to_high,
    z_pair, z_from_low, z_from_high, z_to_low, z_to_high,
):
    high, low = split(x[...].T)
    x_pair[:, : high.shape[1]] = high
    x_pair[:, high.shape[1] :] = low
    window = split(y[...])
    y_full[...] = stacked(window, shard_y, BY, shard_y + 2 * BY, 0, 1)
    y_local[...] = stacked(window, shard_y, BY, shard_y, BY, 1)
    y_to_low[...] = stacked(window, BY, 0, BY, BY, 1)
    y_to_high[...] = stacked(window, BY, shard_y + BY, BY, shard_y, 1)
    window = split(z[...])
    rows = shard_z * GROUP
    for at in range(2):
        block, _ = picked(window[at], shard_z, BAND, shard_z, BAND, GROUP, 1)
        z_pair[at * rows : (at + 1) * rows, :] = block.astype(jnp.bfloat16)
    z_from_low[...] = stacked(window, BAND, BAND, BAND, 0, GROUP)
    z_from_high[...] = stacked(window, BAND, shard_z, BAND, shard_z + BAND, GROUP)
    z_to_low[...] = stacked(window, BAND, 0, BAND, BAND, GROUP)
    z_to_high[...] = stacked(window, BAND, shard_z + BAND, BAND, shard_z, GROUP)


def window(matrix, first, shard, halo):
    return lax.dynamic_slice(jnp.pad(matrix, halo), (first, first), (shard + 2 * halo,) * 2)


def matrices(deriv_x, deriv_y, deriv_z, shard_z, shard_y):
    extent = deriv_x.shape[0]
    z = window(deriv_z, lax.axis_index("wide") * shard_z, shard_z, BAND)
    y = window(deriv_y, lax.axis_index("narrow") * shard_y, shard_y, BY)
    edge = 2 * BAND * GROUP
    rows = shard_z * GROUP
    shapes = [
        (extent, 2 * extent),
        (2 * shard_y, 2 * (shard_y + 2 * BY)),
        (2 * shard_y, 2 * shard_y),
        (2 * BY, 2 * BY),
        (2 * BY, 2 * BY),
        (2 * rows, rows),
    ] + [(edge, edge)] * 4
    out = pl.pallas_call(
        functools.partial(matrices_kernel, shard_z, shard_y),
        out_shape=[jax.ShapeDtypeStruct(shape, jnp.bfloat16) for shape in shapes],
        compiler_params=params(),
        cost_estimate=cost(1e8, 4e6),
        name="matrices",
    )(deriv_x, y, z)
    return out[:5], out[5], out[6:8], out[8:10]


def apply_stacked(matrix, values):
    product = dot(matrix, jnp.concatenate(split(values), axis=0))
    rows = product.shape[0] // 2
    return product[:rows] + product[rows:]


def turbine_kernel(
    count, shard, zs, ys, xs, thrust, a0, a1, u0, weight, source, grad0, grad1
):
    shard_z, shard_y, planes = shard
    step = pl.program_id(0)

    @pl.when(step == 0)
    def _():
        source[...] = jnp.zeros_like(source)

    grad0[...] = jnp.zeros_like(grad0)
    grad1[...] = jnp.zeros_like(grad1)
    for slot in range(count):
        turbine = step * count + slot
        first_z = zs[turbine]
        low = jnp.maximum(first_z, 0)
        high = jnp.minimum(first_z + planes, shard_z)
        lanes = pl.ds(pl.multiple_of(xs[turbine] * 128, 128), 128)
        for line in range(RY):
            y = ys[turbine] + line

            @pl.when((y >= 0) & (y < shard_y) & (high > low))
            def _():
                tile = pl.ds(pl.multiple_of(y // 8 * 8, 8), 8)
                chosen = lax.broadcasted_iota(jnp.int32, (8, 128), 0) == y % 8

                def body(z, sums):
                    row = weight[slot, pl.ds((z - first_z) * RY + line, 1), :]
                    row = jnp.where(chosen, jnp.broadcast_to(row, (8, 128)), 0.0)
                    at = (z, tile, lanes)
                    u = u0[at]
                    driven = row * u * jnp.abs(u)
                    source[at] += row * thrust[turbine]
                    return sums[0] + driven * a0[at], sums[1] + driven * a1[at]

                zero = jnp.zeros((8, 128), jnp.float32)
                sums = lax.fori_loop(low, high, body, (zero, zero))
                grad0[slot : slot + 1, :] += jnp.sum(sums[0], axis=0, keepdims=True)
                grad1[slot : slot + 1, :] += jnp.sum(sums[1], axis=0, keepdims=True)


def turbine_terms(adjoint, velocity, rotor_blocks, disk_weight, thrust):
    _, shard_z, shard_y, extent = adjoint.shape
    x_blocks = extent // 128
    turbines, blocks = rotor_blocks.shape
    count = 8
    first = rotor_blocks[:, 0]
    line = first // x_blocks
    zs = line // NY - lax.axis_index("wide") * shard_z
    ys = line % NY - lax.axis_index("narrow") * shard_y
    xs = first % x_blocks
    field = lambda c: pl.BlockSpec((None, shard_z, shard_y, extent), lambda i, *_: (c, 0, 0, 0))
    sums = pl.BlockSpec((count, 128), lambda i, *_: (i, 0))
    return pl.pallas_call(
        functools.partial(turbine_kernel, count, (shard_z, shard_y, blocks // RY)),
        grid_spec=pltpu.PrefetchScalarGridSpec(
            num_scalar_prefetch=4,
            grid=(turbines // count,),
            in_specs=[
                field(0),
                field(1),
                field(0),
                pl.BlockSpec((count, blocks, 128), lambda i, *_: (i, 0, 0)),
            ],
            out_specs=[
                pl.BlockSpec((shard_z, shard_y, extent), lambda i, *_: (0, 0, 0)),
                sums,
                sums,
            ],
        ),
        out_shape=[
            jax.ShapeDtypeStruct((shard_z, shard_y, extent), jnp.float32),
            jax.ShapeDtypeStruct((turbines, 128), jnp.float32),
            jax.ShapeDtypeStruct((turbines, 128), jnp.float32),
        ],
        compiler_params=params(),
        cost_estimate=cost(1e6, 3e7),
        name="turbine_terms",
    )(zs, ys, xs, thrust, adjoint, adjoint, velocity, disk_weight)


def z_local_kernel(matrix, adjoint, velocity, out):
    _, shard_z, group, extent = adjoint.shape
    rows = shard_z * group
    both = matrix[...]
    high_part = both[:rows]

    def derivative(values):
        high, low = split(values.reshape(rows, extent))
        wide = dot(both, high)
        total = wide[:rows] + wide[rows:] + dot(high_part, low)
        return total.reshape(shard_z, group, extent)

    carrier = velocity[2]
    stretch = adjoint[0] * derivative(velocity[0])
    stretch += adjoint[1] * derivative(velocity[1])
    stretch += adjoint[2] * derivative(velocity[2])
    out[0] = carrier * derivative(adjoint[0])
    out[1] = carrier * derivative(adjoint[1])
    out[2] = carrier * derivative(adjoint[2]) - stretch


def z_local(matrix, adjoint, velocity):
    _, shard_z, shard_y, extent = adjoint.shape
    block = pl.BlockSpec((3, shard_z, GROUP, extent), lambda i: (0, 0, i, 0))
    return pl.pallas_call(
        z_local_kernel,
        grid=(shard_y // GROUP,),
        in_specs=[pl.BlockSpec(matrix.shape, lambda i: (0, 0)), block, block],
        out_specs=block,
        out_shape=jax.ShapeDtypeStruct(adjoint.shape, jnp.float32),
        compiler_params=params(),
        cost_estimate=cost(2e10, 4e7),
        name="z_local",
    )(matrix, adjoint, velocity)


def xy_kernel(
    matrix_x, matrix_ya, matrix_yv, edge_low, edge_high,
    adjoint, velocity, halo_low, halo_high, source, tendency, out, back_low, back_high,
):
    _, planes, shard_y, extent = adjoint.shape
    rows = planes * shard_y
    x_high = matrix_x[:, :extent]
    x_low = matrix_x[:, extent:]

    def along_x(values):
        high, low = split(values.reshape(rows, extent))
        total = dot(high, x_high) + (dot(low, x_high) + dot(high, x_low))
        return total.reshape(planes, shard_y, extent)

    a0, a1, a2 = adjoint[0], adjoint[1], adjoint[2]
    u = velocity[0]
    stretch = a0 * along_x(velocity[0])
    stretch += a1 * along_x(velocity[1])
    stretch += a2 * along_x(velocity[2])
    out[0] = tendency[0] + u * along_x(a0) - stretch - source[...] * jnp.abs(u) * a0
    out[1] = tendency[1] + u * along_x(a1)
    out[2] = tendency[2] + u * along_x(a2)
    for plane in range(planes):
        stretch = jnp.zeros((shard_y, extent), jnp.float32)
        low_sum = jnp.zeros((BY, extent), jnp.float32)
        high_sum = jnp.zeros((BY, extent), jnp.float32)
        carrier = velocity[1, plane]
        for c in range(3):
            value = velocity[c, plane]
            here = adjoint[c, plane]
            below = halo_low[c, plane]
            above = halo_high[c, plane]
            stretch += here * apply_stacked(matrix_yv[...], value)
            low_sum += below * apply_stacked(edge_low[...], value[:BY])
            high_sum += above * apply_stacked(edge_high[...], value[shard_y - BY :])
            column = jnp.concatenate([below, here, above], axis=0)
            out[c, plane] += carrier * apply_stacked(matrix_ya[...], column)
        out[1, plane] -= stretch
        back_low[plane] = low_sum
        back_high[plane] = high_sum


def xy_terms(operators, adjoint, velocity, halo_low, halo_high, source, tendency):
    _, shard_z, shard_y, extent = adjoint.shape
    planes = 4
    whole = lambda m: pl.BlockSpec(m.shape, lambda i: (0, 0))
    block = pl.BlockSpec((3, planes, shard_y, extent), lambda i: (0, i, 0, 0))
    halo = pl.BlockSpec((3, planes, BY, extent), lambda i: (0, i, 0, 0))
    back = pl.BlockSpec((planes, BY, extent), lambda i: (i, 0, 0))
    plane = pl.BlockSpec((planes, shard_y, extent), lambda i: (i, 0, 0))
    back_shape = jax.ShapeDtypeStruct((shard_z, BY, extent), jnp.float32)
    return pl.pallas_call(
        xy_kernel,
        grid=(shard_z // planes,),
        in_specs=[whole(m) for m in operators] + [block, block, halo, halo, plane, block],
        out_specs=[block, back, back],
        out_shape=[jax.ShapeDtypeStruct(adjoint.shape, jnp.float32), back_shape, back_shape],
        compiler_params=params(),
        cost_estimate=cost(2e10, 7e7),
        name="xy_terms",
    )(*operators, adjoint, velocity, halo_low, halo_high, source, tendency)


def z_back_kernel(edge_low, edge_high, vel_low, vel_high, halo_low, halo_high, back_low, back_high):
    _, band, group, extent = vel_low.shape
    rows = band * group
    for edge, vel, halo, back in (
        (edge_low, vel_low, halo_low, back_low),
        (edge_high, vel_high, halo_high, back_high),
    ):
        total = jnp.zeros((rows, extent), jnp.float32)
        for c in range(3):
            value = vel[c].reshape(rows, extent)
            total += halo[c].reshape(rows, extent) * apply_stacked(edge[...], value)
        back[...] = total.reshape(band, group, extent)


def z_back(edge_low, edge_high, velocity, halo_low, halo_high):
    _, shard_z, shard_y, extent = velocity.shape
    last = shard_z // BAND - 1
    whole = lambda m: pl.BlockSpec(m.shape, lambda i: (0, 0))
    edge = lambda at: pl.BlockSpec((3, BAND, GROUP, extent), lambda i: (0, at, i, 0))
    back = pl.BlockSpec((BAND, GROUP, extent), lambda i: (0, i, 0))
    shape = jax.ShapeDtypeStruct((BAND, shard_y, extent), jnp.float32)
    return pl.pallas_call(
        z_back_kernel,
        grid=(shard_y // GROUP,),
        in_specs=[whole(edge_low), whole(edge_high), edge(0), edge(last), edge(0), edge(0)],
        out_specs=[back, back],
        out_shape=[shape, shape],
        compiler_params=params(52 * 1024 * 1024),
        cost_estimate=cost(3e9, 2e7),
        name="z_back",
    )(edge_low, edge_high, velocity, velocity, halo_low, halo_high)


def combine_kernel(
    from_low, from_high, adjoint, carrier, tendency, halo_low, halo_high, stretch_y, out
):
    _, shard_z, group, extent = adjoint.shape
    rows = BAND * group
    top = shard_z - BAND
    for c in range(3):
        total = tendency[c]
        if c == 1:
            total = total - stretch_y[...]
        out[c] = adjoint[c] + STEP * total
        for matrix, halo, at in ((from_low, halo_low, 0), (from_high, halo_high, top)):
            part = apply_stacked(matrix[...], halo[c].reshape(rows, extent))
            planes = slice(at, at + BAND)
            out[c, planes] += STEP * (carrier[planes] * part.reshape(BAND, group, extent))


def combine(from_low, from_high, adjoint, velocity, tendency, halo_low, halo_high, stretch_y):
    _, shard_z, shard_y, extent = adjoint.shape
    whole = lambda m: pl.BlockSpec(m.shape, lambda i: (0, 0))
    block = pl.BlockSpec((3, shard_z, GROUP, extent), lambda i: (0, 0, i, 0))
    carrier = pl.BlockSpec((None, shard_z, GROUP, extent), lambda i: (2, 0, i, 0))
    halo = pl.BlockSpec((3, BAND, GROUP, extent), lambda i: (0, 0, i, 0))
    plane = pl.BlockSpec((shard_z, GROUP, extent), lambda i: (0, i, 0))
    return pl.pallas_call(
        combine_kernel,
        grid=(shard_y // GROUP,),
        in_specs=[whole(from_low), whole(from_high), block, carrier, block, halo, halo, plane],
        out_specs=block,
        out_shape=jax.ShapeDtypeStruct(adjoint.shape, jnp.float32),
        compiler_params=params(),
        cost_estimate=cost(3e9, 5e7),
        name="combine",
    )(from_low, from_high, adjoint, velocity, tendency, halo_low, halo_high, stretch_y)


def finish_kernel(back_low, back_high, updated, out):
    back = jnp.where(pl.program_id(0) == 0, back_low[...], back_high[...])
    out[...] = updated[...] - STEP * back


def finish(updated, back_low, back_high):
    _, shard_z, shard_y, extent = updated.shape
    last = shard_z // BAND - 1
    lines = shard_y // 2
    edge = pl.BlockSpec((None, BAND, lines, extent), lambda i, j: (2, i * last, j, 0))
    back = pl.BlockSpec((BAND, lines, extent), lambda i, j: (0, j, 0))
    return pl.pallas_call(
        finish_kernel,
        grid=(2, shard_y // lines),
        in_specs=[back, back, edge],
        out_specs=edge,
        out_shape=jax.ShapeDtypeStruct(updated.shape, jnp.float32),
        input_output_aliases={2: 0},
        compiler_params=params(8 * 1024 * 1024),
        cost_estimate=cost(1e6, 6e6),
        name="finish",
    )(back_low, back_high, updated)


def send_up(value, axis):
    size = lax.axis_size(axis)
    return lax.ppermute(value, axis, [(i, i + 1) for i in range(size - 1)])


def send_down(value, axis):
    size = lax.axis_size(axis)
    return lax.ppermute(value, axis, [(i + 1, i) for i in range(size - 1)])


def exchange(value, axis, distance):
    size = lax.axis_size(axis)
    return lax.ppermute(value, axis, [(i, i ^ distance) for i in range(size)])


def after(value, *others):
    return lax.optimization_barrier((value, *others))


def owner_rows(grad, turbine_owner):
    turbines = turbine_owner.shape[0]
    devices = lax.axis_size("wide") * lax.axis_size("narrow")
    slot_count = (turbines - 2) // devices + 2
    device = lax.axis_index("wide") * lax.axis_size("narrow") + lax.axis_index("narrow")
    positions = jnp.arange(turbines)
    shared = turbine_owner[:, None] == turbine_owner[None, :]
    earlier = positions[:, None] > positions[None, :]
    slot_rank = jnp.sum((shared & earlier).astype(jnp.int32), axis=1)
    mine = (turbine_owner[None, :] == device) & (jnp.arange(slot_count)[:, None] == slot_rank[None, :])
    return jnp.sum(jnp.where(mine[:, None, :], grad[None], 0.0), axis=2)


def on_device(
    adjoint, velocity, deriv_x, deriv_y, deriv_z, rotor_blocks, turbine_owner, disk_weight, thrust
):
    _, shard_z, shard_y, extent = adjoint.shape
    top, bottom, adjoint = after(adjoint[:, shard_z - BAND :], adjoint[:, :BAND], adjoint)
    z_low = send_up(top, "wide")
    z_high = send_down(bottom, "wide")
    y_low = send_up(adjoint[:, :, shard_y - BY :], "narrow")
    y_high = send_down(adjoint[:, :, :BY], "narrow")

    steps = [("narrow", 2**k) for k in range(8) if 2**k < lax.axis_size("narrow")]
    steps += [("wide", 2**k) for k in range(8) if 2**k < lax.axis_size("wide")]

    source, grad0, grad1 = turbine_terms(adjoint, velocity, rotor_blocks, disk_weight, thrust)
    scale = 1.0 / math.sqrt(128.0 * rotor_blocks.shape[1])
    grad = jnp.stack([jnp.sum(grad0, axis=1), jnp.sum(grad1, axis=1)]) * scale
    xy_matrices, z_pair, z_from, z_to = matrices(deriv_x, deriv_y, deriv_z, shard_z, shard_y)

    moved = exchange(grad, *steps[0])
    tendency = z_local(z_pair, adjoint, velocity)
    moved, tendency = after(moved, tendency)
    grad = grad + moved
    moved = exchange(grad, *steps[1])
    moved, y_low, y_high = after(moved, y_low, y_high)
    grad = grad + moved
    moved = exchange(grad, *steps[2])
    tendency, y_back_low, y_back_high = xy_terms(
        xy_matrices, adjoint, velocity, y_low, y_high, source, tendency
    )
    stretch_low = send_up(y_back_high, "narrow")
    stretch_high = send_down(y_back_low, "narrow")
    moved, tendency, z_low, z_high = after(moved, tendency, z_low, z_high)
    grad = grad + moved
    z_back_low, z_back_high = z_back(*z_to, velocity, z_low, z_high)
    last_low = send_up(z_back_high, "wide")
    last_high = send_down(z_back_low, "wide")
    moved = exchange(grad, *steps[3])
    rest = shard_y - BY
    stretch_y = jnp.pad(stretch_low, ((0, 0), (0, rest), (0, 0))) + jnp.pad(
        stretch_high, ((0, 0), (rest, 0), (0, 0))
    )
    updated = combine(*z_from, adjoint, velocity, tendency, z_low, z_high, stretch_y)
    moved, updated = after(moved, updated)
    grad = grad + moved
    for step in steps[4:]:
        grad = grad + exchange(grad, *step)
    return finish(updated, last_low, last_high), owner_rows(grad, turbine_owner)


def solution(mesh):
    return jax.shard_map(
        on_device,
        mesh=mesh,
        in_specs=(
            P(None, "wide", "narrow", None),
            P(None, "wide", "narrow", None),
            P(),
            P(),
            P(),
            P(),
            P(),
            P(),
            P(),
        ),
        out_specs=(P(None, "wide", "narrow", None), P(("wide", "narrow"), None)),
        check_vma=False,
    )
```

```python
import functools
import math

import jax
import jax.numpy as jnp
from jax import lax
from jax.experimental import pallas as pl
from jax.experimental.pallas import tpu as pltpu
from jax.sharding import PartitionSpec as P

NY = 256
BY = 32
BAND = 16
RY = 2
STEP = 0.2
GROUP = 8
VMEM = 56 * 1024 * 1024


def params(limit=VMEM):
    return pltpu.CompilerParams(vmem_limit_bytes=limit)


def cost(flops, moved):
    return pl.CostEstimate(flops=int(flops / 50), bytes_accessed=int(moved / 50), transcendentals=0)


def split(value):
    high = value.astype(jnp.bfloat16)
    low = (value - high.astype(jnp.float32)).astype(jnp.bfloat16)
    return high, low


def dot(left, right):
    return jnp.dot(left, right, preferred_element_type=jnp.float32)


def picked(window, rows, first_row, columns, first_column, repeat, copies):
    size = window.shape[0]
    height, width = rows * repeat, columns * repeat * copies
    i = lax.broadcasted_iota(jnp.int32, (height, size), 0)
    k = lax.broadcasted_iota(jnp.int32, (height, size), 1)
    left = (lax.div(i, repeat) + first_row == k).astype(jnp.float32).astype(jnp.bfloat16)
    k = lax.broadcasted_iota(jnp.int32, (size, width), 0)
    j = lax.rem(lax.broadcasted_iota(jnp.int32, (size, width), 1), columns * repeat)
    right = (lax.div(j, repeat) + first_column == k).astype(jnp.float32).astype(jnp.bfloat16)
    block = dot(dot(left, window).astype(jnp.bfloat16), right)
    i = lax.broadcasted_iota(jnp.int32, (height, width), 0)
    j = lax.broadcasted_iota(jnp.int32, (height, width), 1)
    return jnp.where(lax.rem(i, repeat) == lax.rem(j, repeat), block, 0.0), j


def stacked(window, rows, first_row, columns, first_column, repeat):
    high, low = window
    top, j = picked(high, rows, first_row, columns, first_column, repeat, 2)
    bottom, _ = picked(low, rows, first_row, columns, first_column, repeat, 2)
    bottom = jnp.where(j < columns * repeat, bottom, 0.0)
    return jnp.concatenate([top, bottom], axis=0).astype(jnp.bfloat16)


def matrices_kernel(
    shard_z, shard_y, x, y, z,
    x_pair, y_full, y_local, y_to_low, y_to_high,
    z_pair, z_from_low, z_from_high, z_to_low, z_to_high,
):
    high, low = split(x[...].T)
    x_pair[:, : high.shape[1]] = high
    x_pair[:, high.shape[1] :] = low
    window = split(y[...])
    y_full[...] = stacked(window, shard_y, BY, shard_y + 2 * BY, 0, 1)
    y_local[...] = stacked(window, shard_y, BY, shard_y, BY, 1)
    y_to_low[...] = stacked(window, BY, 0, BY, BY, 1)
    y_to_high[...] = stacked(window, BY, shard_y + BY, BY, shard_y, 1)
    window = split(z[...])
    rows = shard_z * GROUP
    for at in range(2):
        block, _ = picked(window[at], shard_z, BAND, shard_z, BAND, GROUP, 1)
        z_pair[at * rows : (at + 1) * rows, :] = block.astype(jnp.bfloat16)
    z_from_low[...] = stacked(window, BAND, BAND, BAND, 0, GROUP)
    z_from_high[...] = stacked(window, BAND, shard_z, BAND, shard_z + BAND, GROUP)
    z_to_low[...] = stacked(window, BAND, 0, BAND, BAND, GROUP)
    z_to_high[...] = stacked(window, BAND, shard_z + BAND, BAND, shard_z, GROUP)


def window(matrix, first, shard, halo):
    return lax.dynamic_slice(jnp.pad(matrix, halo), (first, first), (shard + 2 * halo,) * 2)


def matrices(deriv_x, deriv_y, deriv_z, shard_z, shard_y):
    extent = deriv_x.shape[0]
    z = window(deriv_z, lax.axis_index("wide") * shard_z, shard_z, BAND)
    y = window(deriv_y, lax.axis_index("narrow") * shard_y, shard_y, BY)
    edge = 2 * BAND * GROUP
    rows = shard_z * GROUP
    shapes = [
        (extent, 2 * extent),
        (2 * shard_y, 2 * (shard_y + 2 * BY)),
        (2 * shard_y, 2 * shard_y),
        (2 * BY, 2 * BY),
        (2 * BY, 2 * BY),
        (2 * rows, rows),
    ] + [(edge, edge)] * 4
    out = pl.pallas_call(
        functools.partial(matrices_kernel, shard_z, shard_y),
        out_shape=[jax.ShapeDtypeStruct(shape, jnp.bfloat16) for shape in shapes],
        compiler_params=params(),
        cost_estimate=cost(1e8, 4e6),
        name="matrices",
    )(deriv_x, y, z)
    return out[:5], out[5], out[6:8], out[8:10]


def apply_stacked(matrix, values):
    product = dot(matrix, jnp.concatenate(split(values), axis=0))
    rows = product.shape[0] // 2
    return product[:rows] + product[rows:]


def turbine_kernel(
    count, shard, zs, ys, xs, thrust, a0, a1, u0, weight, source, grad0, grad1
):
    shard_z, shard_y, planes = shard
    step = pl.program_id(0)

    @pl.when(step == 0)
    def _():
        source[...] = jnp.zeros_like(source)

    grad0[...] = jnp.zeros_like(grad0)
    grad1[...] = jnp.zeros_like(grad1)
    for slot in range(count):
        turbine = step * count + slot
        first_z = zs[turbine]
        low = jnp.maximum(first_z, 0)
        high = jnp.minimum(first_z + planes, shard_z)
        lanes = pl.ds(pl.multiple_of(xs[turbine] * 128, 128), 128)
        for line in range(RY):
            y = ys[turbine] + line

            @pl.when((y >= 0) & (y < shard_y) & (high > low))
            def _():
                tile = pl.ds(pl.multiple_of(y // 8 * 8, 8), 8)
                chosen = lax.broadcasted_iota(jnp.int32, (8, 128), 0) == y % 8

                def body(z, sums):
                    row = weight[slot, pl.ds((z - first_z) * RY + line, 1), :]
                    row = jnp.where(chosen, jnp.broadcast_to(row, (8, 128)), 0.0)
                    at = (z, tile, lanes)
                    u = u0[at]
                    driven = row * u * jnp.abs(u)
                    source[at] += row * thrust[turbine]
                    return sums[0] + driven * a0[at], sums[1] + driven * a1[at]

                zero = jnp.zeros((8, 128), jnp.float32)
                sums = lax.fori_loop(low, high, body, (zero, zero))
                grad0[slot : slot + 1, :] += jnp.sum(sums[0], axis=0, keepdims=True)
                grad1[slot : slot + 1, :] += jnp.sum(sums[1], axis=0, keepdims=True)


def turbine_terms(adjoint, velocity, rotor_blocks, disk_weight, thrust):
    _, shard_z, shard_y, extent = adjoint.shape
    x_blocks = extent // 128
    turbines, blocks = rotor_blocks.shape
    count = 8
    first = rotor_blocks[:, 0]
    line = first // x_blocks
    zs = line // NY - lax.axis_index("wide") * shard_z
    ys = line % NY - lax.axis_index("narrow") * shard_y
    xs = first % x_blocks
    field = lambda c: pl.BlockSpec((None, shard_z, shard_y, extent), lambda i, *_: (c, 0, 0, 0))
    sums = pl.BlockSpec((count, 128), lambda i, *_: (i, 0))
    return pl.pallas_call(
        functools.partial(turbine_kernel, count, (shard_z, shard_y, blocks // RY)),
        grid_spec=pltpu.PrefetchScalarGridSpec(
            num_scalar_prefetch=4,
            grid=(turbines // count,),
            in_specs=[
                field(0),
                field(1),
                field(0),
                pl.BlockSpec((count, blocks, 128), lambda i, *_: (i, 0, 0)),
            ],
            out_specs=[
                pl.BlockSpec((shard_z, shard_y, extent), lambda i, *_: (0, 0, 0)),
                sums,
                sums,
            ],
        ),
        out_shape=[
            jax.ShapeDtypeStruct((shard_z, shard_y, extent), jnp.float32),
            jax.ShapeDtypeStruct((turbines, 128), jnp.float32),
            jax.ShapeDtypeStruct((turbines, 128), jnp.float32),
        ],
        compiler_params=params(),
        cost_estimate=cost(1e6, 3e7),
        name="turbine_terms",
    )(zs, ys, xs, thrust, adjoint, adjoint, velocity, disk_weight)


def z_local_kernel(matrix, adjoint, velocity, out):
    _, shard_z, group, extent = adjoint.shape
    rows = shard_z * group
    both = matrix[...]
    high_part = both[:rows]

    def derivative(values):
        high, low = split(values.reshape(rows, extent))
        wide = dot(both, high)
        total = wide[:rows] + wide[rows:] + dot(high_part, low)
        return total.reshape(shard_z, group, extent)

    carrier = velocity[2]
    stretch = adjoint[0] * derivative(velocity[0])
    stretch += adjoint[1] * derivative(velocity[1])
    stretch += adjoint[2] * derivative(velocity[2])
    out[0] = carrier * derivative(adjoint[0])
    out[1] = carrier * derivative(adjoint[1])
    out[2] = carrier * derivative(adjoint[2]) - stretch


def z_local(matrix, adjoint, velocity):
    _, shard_z, shard_y, extent = adjoint.shape
    block = pl.BlockSpec((3, shard_z, GROUP, extent), lambda i: (0, 0, i, 0))
    return pl.pallas_call(
        z_local_kernel,
        grid=(shard_y // GROUP,),
        in_specs=[pl.BlockSpec(matrix.shape, lambda i: (0, 0)), block, block],
        out_specs=block,
        out_shape=jax.ShapeDtypeStruct(adjoint.shape, jnp.float32),
        compiler_params=params(),
        cost_estimate=cost(2e10, 4e7),
        name="z_local",
    )(matrix, adjoint, velocity)


def xy_kernel(
    matrix_x, matrix_ya, matrix_yv, edge_low, edge_high,
    adjoint, velocity, halo_low, halo_high, source, tendency, out, back_low, back_high,
):
    _, planes, shard_y, extent = adjoint.shape
    rows = planes * shard_y
    x_high = matrix_x[:, :extent]
    x_low = matrix_x[:, extent:]

    def along_x(values):
        high, low = split(values.reshape(rows, extent))
        total = dot(high, x_high) + (dot(low, x_high) + dot(high, x_low))
        return total.reshape(planes, shard_y, extent)

    a0, a1, a2 = adjoint[0], adjoint[1], adjoint[2]
    u = velocity[0]
    stretch = a0 * along_x(velocity[0])
    stretch += a1 * along_x(velocity[1])
    stretch += a2 * along_x(velocity[2])
    out[0] = tendency[0] + u * along_x(a0) - stretch - source[...] * jnp.abs(u) * a0
    out[1] = tendency[1] + u * along_x(a1)
    out[2] = tendency[2] + u * along_x(a2)
    for plane in range(planes):
        stretch = jnp.zeros((shard_y, extent), jnp.float32)
        low_sum = jnp.zeros((BY, extent), jnp.float32)
        high_sum = jnp.zeros((BY, extent), jnp.float32)
        carrier = velocity[1, plane]
        for c in range(3):
            value = velocity[c, plane]
            here = adjoint[c, plane]
            below = halo_low[c, plane]
            above = halo_high[c, plane]
            stretch += here * apply_stacked(matrix_yv[...], value)
            low_sum += below * apply_stacked(edge_low[...], value[:BY])
            high_sum += above * apply_stacked(edge_high[...], value[shard_y - BY :])
            column = jnp.concatenate([below, here, above], axis=0)
            out[c, plane] += carrier * apply_stacked(matrix_ya[...], column)
        out[1, plane] -= stretch
        back_low[plane] = low_sum
        back_high[plane] = high_sum


def xy_terms(operators, adjoint, velocity, halo_low, halo_high, source, tendency):
    _, shard_z, shard_y, extent = adjoint.shape
    planes = 4
    whole = lambda m: pl.BlockSpec(m.shape, lambda i: (0, 0))
    block = pl.BlockSpec((3, planes, shard_y, extent), lambda i: (0, i, 0, 0))
    halo = pl.BlockSpec((3, planes, BY, extent), lambda i: (0, i, 0, 0))
    back = pl.BlockSpec((planes, BY, extent), lambda i: (i, 0, 0))
    plane = pl.BlockSpec((planes, shard_y, extent), lambda i: (i, 0, 0))
    back_shape = jax.ShapeDtypeStruct((shard_z, BY, extent), jnp.float32)
    return pl.pallas_call(
        xy_kernel,
        grid=(shard_z // planes,),
        in_specs=[whole(m) for m in operators] + [block, block, halo, halo, plane, block],
        out_specs=[block, back, back],
        out_shape=[jax.ShapeDtypeStruct(adjoint.shape, jnp.float32), back_shape, back_shape],
        compiler_params=params(),
        cost_estimate=cost(2e10, 7e7),
        name="xy_terms",
    )(*operators, adjoint, velocity, halo_low, halo_high, source, tendency)


def z_back_kernel(edge_low, edge_high, vel_low, vel_high, halo_low, halo_high, back_low, back_high):
    _, band, lines, extent = vel_low.shape
    rows = band * GROUP
    for edge, vel, halo, back in (
        (edge_low, vel_low, halo_low, back_low),
        (edge_high, vel_high, halo_high, back_high),
    ):
        for first in range(0, lines, GROUP):
            at = slice(first, first + GROUP)
            total = jnp.zeros((rows, extent), jnp.float32)
            for c in range(3):
                value = vel[c, :, at].reshape(rows, extent)
                total += halo[c, :, at].reshape(rows, extent) * apply_stacked(edge[...], value)
            back[:, at] = total.reshape(band, GROUP, extent)


def z_back(edge_low, edge_high, velocity, halo_low, halo_high):
    _, shard_z, shard_y, extent = velocity.shape
    last = shard_z // BAND - 1
    lines = 2 * GROUP
    whole = lambda m: pl.BlockSpec(m.shape, lambda i: (0, 0))
    edge = lambda at: pl.BlockSpec((3, BAND, lines, extent), lambda i: (0, at, i, 0))
    back = pl.BlockSpec((BAND, lines, extent), lambda i: (0, i, 0))
    shape = jax.ShapeDtypeStruct((BAND, shard_y, extent), jnp.float32)
    return pl.pallas_call(
        z_back_kernel,
        grid=(shard_y // lines,),
        in_specs=[whole(edge_low), whole(edge_high), edge(0), edge(last), edge(0), edge(0)],
        out_specs=[back, back],
        out_shape=[shape, shape],
        compiler_params=params(52 * 1024 * 1024),
        cost_estimate=cost(3e9, 2e7),
        name="z_back",
    )(edge_low, edge_high, velocity, velocity, halo_low, halo_high)


def combine_kernel(
    from_low, from_high, adjoint, carrier, tendency, halo_low, halo_high, stretch_y, out
):
    _, shard_z, group, extent = adjoint.shape
    rows = BAND * group
    top = shard_z - BAND
    for c in range(3):
        total = tendency[c]
        if c == 1:
            total = total - stretch_y[...]
        out[c] = adjoint[c] + STEP * total
        for matrix, halo, at in ((from_low, halo_low, 0), (from_high, halo_high, top)):
            part = apply_stacked(matrix[...], halo[c].reshape(rows, extent))
            planes = slice(at, at + BAND)
            out[c, planes] += STEP * (carrier[planes] * part.reshape(BAND, group, extent))


def combine(from_low, from_high, adjoint, velocity, tendency, halo_low, halo_high, stretch_y):
    _, shard_z, shard_y, extent = adjoint.shape
    whole = lambda m: pl.BlockSpec(m.shape, lambda i: (0, 0))
    block = pl.BlockSpec((3, shard_z, GROUP, extent), lambda i: (0, 0, i, 0))
    carrier = pl.BlockSpec((None, shard_z, GROUP, extent), lambda i: (2, 0, i, 0))
    halo = pl.BlockSpec((3, BAND, GROUP, extent), lambda i: (0, 0, i, 0))
    plane = pl.BlockSpec((shard_z, GROUP, extent), lambda i: (0, i, 0))
    return pl.pallas_call(
        combine_kernel,
        grid=(shard_y // GROUP,),
        in_specs=[whole(from_low), whole(from_high), block, carrier, block, halo, halo, plane],
        out_specs=block,
        out_shape=jax.ShapeDtypeStruct(adjoint.shape, jnp.float32),
        compiler_params=params(),
        cost_estimate=cost(3e9, 5e7),
        name="combine",
    )(from_low, from_high, adjoint, velocity, tendency, halo_low, halo_high, stretch_y)


def finish_kernel(back_low, back_high, updated, out):
    back = jnp.where(pl.program_id(0) == 0, back_low[...], back_high[...])
    out[...] = updated[...] - STEP * back


def finish(updated, back_low, back_high):
    _, shard_z, shard_y, extent = updated.shape
    last = shard_z // BAND - 1
    lines = shard_y // 2
    edge = pl.BlockSpec((None, BAND, lines, extent), lambda i, j: (2, i * last, j, 0))
    back = pl.BlockSpec((BAND, lines, extent), lambda i, j: (0, j, 0))
    return pl.pallas_call(
        finish_kernel,
        grid=(2, shard_y // lines),
        in_specs=[back, back, edge],
        out_specs=edge,
        out_shape=jax.ShapeDtypeStruct(updated.shape, jnp.float32),
        input_output_aliases={2: 0},
        compiler_params=params(8 * 1024 * 1024),
        cost_estimate=cost(1e6, 6e6),
        name="finish",
    )(back_low, back_high, updated)


def edges_kernel(adjoint, top, bottom, left, right, sems):
    _, shard_z, shard_y, _ = adjoint.shape
    copies = [
        pltpu.make_async_copy(adjoint.at[:, pl.ds(shard_z - BAND, BAND)], top, sems.at[0]),
        pltpu.make_async_copy(adjoint.at[:, pl.ds(0, BAND)], bottom, sems.at[1]),
        pltpu.make_async_copy(adjoint.at[:, :, pl.ds(shard_y - BY, BY)], left, sems.at[2]),
        pltpu.make_async_copy(adjoint.at[:, :, pl.ds(0, BY)], right, sems.at[3]),
    ]
    for copy in copies:
        copy.start()
    for copy in copies:
        copy.wait()


def edges(adjoint):
    parts, shard_z, shard_y, extent = adjoint.shape
    planes = jax.ShapeDtypeStruct((parts, BAND, shard_y, extent), jnp.float32)
    lines = jax.ShapeDtypeStruct((parts, shard_z, BY, extent), jnp.float32)
    hbm = pl.BlockSpec(memory_space=pl.ANY)
    return pl.pallas_call(
        edges_kernel,
        in_specs=[hbm],
        out_specs=[hbm] * 4,
        out_shape=[planes, planes, lines, lines],
        scratch_shapes=[pltpu.SemaphoreType.DMA((4,))],
        compiler_params=params(),
        cost_estimate=cost(1e6, 4e7),
        name="edges",
    )(adjoint)


def send_up(value, axis):
    size = lax.axis_size(axis)
    return lax.ppermute(value, axis, [(i, i + 1) for i in range(size - 1)])


def send_down(value, axis):
    size = lax.axis_size(axis)
    return lax.ppermute(value, axis, [(i + 1, i) for i in range(size - 1)])


def exchange(value, axis, distance):
    size = lax.axis_size(axis)
    return lax.ppermute(value, axis, [(i, i ^ distance) for i in range(size)])


def after(value, *others):
    return lax.optimization_barrier((value, *others))


def owner_rows(grad, turbine_owner):
    turbines = turbine_owner.shape[0]
    devices = lax.axis_size("wide") * lax.axis_size("narrow")
    slot_count = (turbines - 2) // devices + 2
    device = lax.axis_index("wide") * lax.axis_size("narrow") + lax.axis_index("narrow")
    positions = jnp.arange(turbines)
    shared = turbine_owner[:, None] == turbine_owner[None, :]
    earlier = positions[:, None] > positions[None, :]
    slot_rank = jnp.sum((shared & earlier).astype(jnp.int32), axis=1)
    mine = (turbine_owner[None, :] == device) & (jnp.arange(slot_count)[:, None] == slot_rank[None, :])
    return jnp.sum(jnp.where(mine[:, None, :], grad[None], 0.0), axis=2)


def on_device(
    adjoint, velocity, deriv_x, deriv_y, deriv_z, rotor_blocks, turbine_owner, disk_weight, thrust
):
    _, shard_z, shard_y, extent = adjoint.shape
    top, bottom, left, right = edges(adjoint)
    z_low = send_up(top, "wide")
    z_high = send_down(bottom, "wide")
    y_low = send_up(left, "narrow")
    y_high = send_down(right, "narrow")

    steps = [("narrow", 2**k) for k in range(8) if 2**k < lax.axis_size("narrow")]
    steps += [("wide", 2**k) for k in range(8) if 2**k < lax.axis_size("wide")]

    source, grad0, grad1 = turbine_terms(adjoint, velocity, rotor_blocks, disk_weight, thrust)
    scale = 1.0 / math.sqrt(128.0 * rotor_blocks.shape[1])
    grad = jnp.stack([jnp.sum(grad0, axis=1), jnp.sum(grad1, axis=1)]) * scale
    xy_matrices, z_pair, z_from, z_to = matrices(deriv_x, deriv_y, deriv_z, shard_z, shard_y)

    moved = exchange(grad, *steps[0])
    tendency = z_local(z_pair, adjoint, velocity)
    moved, tendency = after(moved, tendency)
    grad = grad + moved
    moved = exchange(grad, *steps[1])
    moved, y_low, y_high = after(moved, y_low, y_high)
    grad = grad + moved
    moved = exchange(grad, *steps[2])
    tendency, y_back_low, y_back_high = xy_terms(
        xy_matrices, adjoint, velocity, y_low, y_high, source, tendency
    )
    stretch_low = send_up(y_back_high, "narrow")
    stretch_high = send_down(y_back_low, "narrow")
    moved, tendency, z_low, z_high = after(moved, tendency, z_low, z_high)
    grad = grad + moved
    z_back_low, z_back_high = z_back(*z_to, velocity, z_low, z_high)
    last_low = send_up(z_back_high, "wide")
    last_high = send_down(z_back_low, "wide")
    moved = exchange(grad, *steps[3])
    rest = shard_y - BY
    stretch_y = jnp.pad(stretch_low, ((0, 0), (0, rest), (0, 0))) + jnp.pad(
        stretch_high, ((0, 0), (rest, 0), (0, 0))
    )
    updated = combine(*z_from, adjoint, velocity, tendency, z_low, z_high, stretch_y)
    moved, updated = after(moved, updated)
    grad = grad + moved
    for step in steps[4:]:
        grad = grad + exchange(grad, *step)
    return finish(updated, last_low, last_high), owner_rows(grad, turbine_owner)


def solution(mesh):
    return jax.shard_map(
        on_device,
        mesh=mesh,
        in_specs=(
            P(None, "wide", "narrow", None),
            P(None, "wide", "narrow", None),
            P(),
            P(),
            P(),
            P(),
            P(),
            P(),
            P(),
        ),
        out_specs=(P(None, "wide", "narrow", None), P(("wide", "narrow"), None)),
        check_vma=False,
    )
```

```python
import functools
import math

import jax
import jax.numpy as jnp
from jax import lax
from jax.experimental import pallas as pl
from jax.experimental.pallas import tpu as pltpu
from jax.sharding import PartitionSpec as P

NY = 256
BY = 32
BAND = 16
RY = 2
STEP = 0.2
GROUP = 8
VMEM = 56 * 1024 * 1024


def params(limit=VMEM):
    return pltpu.CompilerParams(vmem_limit_bytes=limit)


def cost(flops, moved):
    return pl.CostEstimate(flops=int(flops / 50), bytes_accessed=int(moved / 50), transcendentals=0)


def split(value):
    high = value.astype(jnp.bfloat16)
    low = (value - high.astype(jnp.float32)).astype(jnp.bfloat16)
    return high, low


def dot(left, right):
    return jnp.dot(left, right, preferred_element_type=jnp.float32)


def picked(window, rows, first_row, columns, first_column, repeat, copies):
    size = window.shape[0]
    height, width = rows * repeat, columns * repeat * copies
    i = lax.broadcasted_iota(jnp.int32, (height, size), 0)
    k = lax.broadcasted_iota(jnp.int32, (height, size), 1)
    left = (lax.div(i, repeat) + first_row == k).astype(jnp.float32).astype(jnp.bfloat16)
    k = lax.broadcasted_iota(jnp.int32, (size, width), 0)
    j = lax.rem(lax.broadcasted_iota(jnp.int32, (size, width), 1), columns * repeat)
    right = (lax.div(j, repeat) + first_column == k).astype(jnp.float32).astype(jnp.bfloat16)
    block = dot(dot(left, window).astype(jnp.bfloat16), right)
    i = lax.broadcasted_iota(jnp.int32, (height, width), 0)
    j = lax.broadcasted_iota(jnp.int32, (height, width), 1)
    return jnp.where(lax.rem(i, repeat) == lax.rem(j, repeat), block, 0.0), j


def stacked(window, rows, first_row, columns, first_column, repeat):
    high, low = window
    top, j = picked(high, rows, first_row, columns, first_column, repeat, 2)
    bottom, _ = picked(low, rows, first_row, columns, first_column, repeat, 2)
    bottom = jnp.where(j < columns * repeat, bottom, 0.0)
    return jnp.concatenate([top, bottom], axis=0).astype(jnp.bfloat16)


def matrices_kernel(
    shard_z, shard_y, x, y, z,
    x_pair, y_full, y_local, y_to_low, y_to_high,
    z_pair, z_from_low, z_from_high, z_to_low, z_to_high,
):
    high, low = split(x[...].T)
    x_pair[:, : high.shape[1]] = high
    x_pair[:, high.shape[1] :] = low
    window = split(y[...])
    y_full[...] = stacked(window, shard_y, BY, shard_y + 2 * BY, 0, 1)
    y_local[...] = stacked(window, shard_y, BY, shard_y, BY, 1)
    y_to_low[...] = stacked(window, BY, 0, BY, BY, 1)
    y_to_high[...] = stacked(window, BY, shard_y + BY, BY, shard_y, 1)
    window = split(z[...])
    rows = shard_z * GROUP
    for at in range(2):
        block, _ = picked(window[at], shard_z, BAND, shard_z, BAND, GROUP, 1)
        z_pair[at * rows : (at + 1) * rows, :] = block.astype(jnp.bfloat16)
    z_from_low[...] = stacked(window, BAND, BAND, BAND, 0, GROUP)
    z_from_high[...] = stacked(window, BAND, shard_z, BAND, shard_z + BAND, GROUP)
    z_to_low[...] = stacked(window, BAND, 0, BAND, BAND, GROUP)
    z_to_high[...] = stacked(window, BAND, shard_z + BAND, BAND, shard_z, GROUP)


def window(matrix, first, shard, halo):
    return lax.dynamic_slice(jnp.pad(matrix, halo), (first, first), (shard + 2 * halo,) * 2)


def matrices(deriv_x, deriv_y, deriv_z, shard_z, shard_y):
    extent = deriv_x.shape[0]
    z = window(deriv_z, lax.axis_index("wide") * shard_z, shard_z, BAND)
    y = window(deriv_y, lax.axis_index("narrow") * shard_y, shard_y, BY)
    edge = 2 * BAND * GROUP
    rows = shard_z * GROUP
    shapes = [
        (extent, 2 * extent),
        (2 * shard_y, 2 * (shard_y + 2 * BY)),
        (2 * shard_y, 2 * shard_y),
        (2 * BY, 2 * BY),
        (2 * BY, 2 * BY),
        (2 * rows, rows),
    ] + [(edge, edge)] * 4
    out = pl.pallas_call(
        functools.partial(matrices_kernel, shard_z, shard_y),
        out_shape=[jax.ShapeDtypeStruct(shape, jnp.bfloat16) for shape in shapes],
        compiler_params=params(),
        cost_estimate=cost(1e8, 4e6),
        name="matrices",
    )(deriv_x, y, z)
    return out[:5], out[5], out[6:8], out[8:10]


def apply_stacked(matrix, values):
    product = dot(matrix, jnp.concatenate(split(values), axis=0))
    rows = product.shape[0] // 2
    return product[:rows] + product[rows:]


def turbine_kernel(
    count, shard, zs, ys, xs, thrust, a0, a1, u0, weight, source, grad0, grad1
):
    shard_z, shard_y, planes = shard
    step = pl.program_id(0)

    @pl.when(step == 0)
    def _():
        source[...] = jnp.zeros_like(source)

    grad0[...] = jnp.zeros_like(grad0)
    grad1[...] = jnp.zeros_like(grad1)
    for slot in range(count):
        turbine = step * count + slot
        first_z = zs[turbine]
        low = jnp.maximum(first_z, 0)
        high = jnp.minimum(first_z + planes, shard_z)
        lanes = pl.ds(pl.multiple_of(xs[turbine] * 128, 128), 128)
        for line in range(RY):
            y = ys[turbine] + line

            @pl.when((y >= 0) & (y < shard_y) & (high > low))
            def _():
                tile = pl.ds(pl.multiple_of(y // 8 * 8, 8), 8)
                chosen = lax.broadcasted_iota(jnp.int32, (8, 128), 0) == y % 8

                def body(z, sums):
                    row = weight[slot, pl.ds((z - first_z) * RY + line, 1), :]
                    row = jnp.where(chosen, jnp.broadcast_to(row, (8, 128)), 0.0)
                    at = (z, tile, lanes)
                    u = u0[at]
                    driven = row * u * jnp.abs(u)
                    source[at] += row * thrust[turbine]
                    return sums[0] + driven * a0[at], sums[1] + driven * a1[at]

                zero = jnp.zeros((8, 128), jnp.float32)
                sums = lax.fori_loop(low, high, body, (zero, zero))
                grad0[slot : slot + 1, :] += jnp.sum(sums[0], axis=0, keepdims=True)
                grad1[slot : slot + 1, :] += jnp.sum(sums[1], axis=0, keepdims=True)


def turbine_terms(adjoint, velocity, rotor_blocks, disk_weight, thrust):
    _, shard_z, shard_y, extent = adjoint.shape
    x_blocks = extent // 128
    turbines, blocks = rotor_blocks.shape
    count = 8
    first = rotor_blocks[:, 0]
    line = first // x_blocks
    zs = line // NY - lax.axis_index("wide") * shard_z
    ys = line % NY - lax.axis_index("narrow") * shard_y
    xs = first % x_blocks
    field = lambda c: pl.BlockSpec((None, shard_z, shard_y, extent), lambda i, *_: (c, 0, 0, 0))
    sums = pl.BlockSpec((count, 128), lambda i, *_: (i, 0))
    return pl.pallas_call(
        functools.partial(turbine_kernel, count, (shard_z, shard_y, blocks // RY)),
        grid_spec=pltpu.PrefetchScalarGridSpec(
            num_scalar_prefetch=4,
            grid=(turbines // count,),
            in_specs=[
                field(0),
                field(1),
                field(0),
                pl.BlockSpec((count, blocks, 128), lambda i, *_: (i, 0, 0)),
            ],
            out_specs=[
                pl.BlockSpec((shard_z, shard_y, extent), lambda i, *_: (0, 0, 0)),
                sums,
                sums,
            ],
        ),
        out_shape=[
            jax.ShapeDtypeStruct((shard_z, shard_y, extent), jnp.float32),
            jax.ShapeDtypeStruct((turbines, 128), jnp.float32),
            jax.ShapeDtypeStruct((turbines, 128), jnp.float32),
        ],
        compiler_params=params(),
        cost_estimate=cost(1e6, 3e7),
        name="turbine_terms",
    )(zs, ys, xs, thrust, adjoint, adjoint, velocity, disk_weight)


def z_local_kernel(matrix, adjoint, velocity, out):
    _, shard_z, group, extent = adjoint.shape
    rows = shard_z * group
    both = matrix[...]
    high_part = both[:rows]

    def derivative(values):
        high, low = split(values.reshape(rows, extent))
        wide = dot(both, high)
        total = wide[:rows] + wide[rows:] + dot(high_part, low)
        return total.reshape(shard_z, group, extent)

    carrier = velocity[2]
    stretch = adjoint[0] * derivative(velocity[0])
    stretch += adjoint[1] * derivative(velocity[1])
    stretch += adjoint[2] * derivative(velocity[2])
    out[0] = carrier * derivative(adjoint[0])
    out[1] = carrier * derivative(adjoint[1])
    out[2] = carrier * derivative(adjoint[2]) - stretch


def z_local(matrix, adjoint, velocity):
    _, shard_z, shard_y, extent = adjoint.shape
    block = pl.BlockSpec((3, shard_z, GROUP, extent), lambda i: (0, 0, i, 0))
    return pl.pallas_call(
        z_local_kernel,
        grid=(shard_y // GROUP,),
        in_specs=[pl.BlockSpec(matrix.shape, lambda i: (0, 0)), block, block],
        out_specs=block,
        out_shape=jax.ShapeDtypeStruct(adjoint.shape, jnp.float32),
        compiler_params=params(),
        cost_estimate=cost(2e10, 4e7),
        name="z_local",
    )(matrix, adjoint, velocity)


def xy_kernel(
    matrix_x, matrix_ya, matrix_yv, edge_low, edge_high,
    adjoint, velocity, halo_low, halo_high, source, tendency, out, back_low, back_high,
):
    _, planes, shard_y, extent = adjoint.shape
    rows = planes * shard_y
    x_high = matrix_x[:, :extent]
    x_low = matrix_x[:, extent:]

    def along_x(values):
        high, low = split(values.reshape(rows, extent))
        total = dot(high, x_high) + (dot(low, x_high) + dot(high, x_low))
        return total.reshape(planes, shard_y, extent)

    a0, a1, a2 = adjoint[0], adjoint[1], adjoint[2]
    u = velocity[0]
    stretch = a0 * along_x(velocity[0])
    stretch += a1 * along_x(velocity[1])
    stretch += a2 * along_x(velocity[2])
    out[0] = tendency[0] + u * along_x(a0) - stretch - source[...] * jnp.abs(u) * a0
    out[1] = tendency[1] + u * along_x(a1)
    out[2] = tendency[2] + u * along_x(a2)
    for plane in range(planes):
        stretch = jnp.zeros((shard_y, extent), jnp.float32)
        low_sum = jnp.zeros((BY, extent), jnp.float32)
        high_sum = jnp.zeros((BY, extent), jnp.float32)
        carrier = velocity[1, plane]
        for c in range(3):
            value = velocity[c, plane]
            here = adjoint[c, plane]
            below = halo_low[c, plane]
            above = halo_high[c, plane]
            stretch += here * apply_stacked(matrix_yv[...], value)
            low_sum += below * apply_stacked(edge_low[...], value[:BY])
            high_sum += above * apply_stacked(edge_high[...], value[shard_y - BY :])
            column = jnp.concatenate([below, here, above], axis=0)
            out[c, plane] += carrier * apply_stacked(matrix_ya[...], column)
        out[1, plane] -= stretch
        back_low[plane] = low_sum
        back_high[plane] = high_sum


def xy_terms(operators, adjoint, velocity, halo_low, halo_high, source, tendency):
    _, shard_z, shard_y, extent = adjoint.shape
    planes = 4
    whole = lambda m: pl.BlockSpec(m.shape, lambda i: (0, 0))
    block = pl.BlockSpec((3, planes, shard_y, extent), lambda i: (0, i, 0, 0))
    halo = pl.BlockSpec((3, planes, BY, extent), lambda i: (0, i, 0, 0))
    back = pl.BlockSpec((planes, BY, extent), lambda i: (i, 0, 0))
    plane = pl.BlockSpec((planes, shard_y, extent), lambda i: (i, 0, 0))
    back_shape = jax.ShapeDtypeStruct((shard_z, BY, extent), jnp.float32)
    return pl.pallas_call(
        xy_kernel,
        grid=(shard_z // planes,),
        in_specs=[whole(m) for m in operators] + [block, block, halo, halo, plane, block],
        out_specs=[block, back, back],
        out_shape=[jax.ShapeDtypeStruct(adjoint.shape, jnp.float32), back_shape, back_shape],
        compiler_params=params(),
        cost_estimate=cost(2e10, 7e7),
        name="xy_terms",
    )(*operators, adjoint, velocity, halo_low, halo_high, source, tendency)


def z_back_kernel(edge_low, edge_high, vel_low, vel_high, halo_low, halo_high, back_low, back_high):
    _, band, lines, extent = vel_low.shape
    rows = band * GROUP
    for edge, vel, halo, back in (
        (edge_low, vel_low, halo_low, back_low),
        (edge_high, vel_high, halo_high, back_high),
    ):
        for first in range(0, lines, GROUP):
            at = slice(first, first + GROUP)
            total = jnp.zeros((rows, extent), jnp.float32)
            for c in range(3):
                value = vel[c, :, at].reshape(rows, extent)
                total += halo[c, :, at].reshape(rows, extent) * apply_stacked(edge[...], value)
            back[:, at] = total.reshape(band, GROUP, extent)


def z_back(edge_low, edge_high, velocity, halo_low, halo_high):
    _, shard_z, shard_y, extent = velocity.shape
    last = shard_z // BAND - 1
    lines = 2 * GROUP
    whole = lambda m: pl.BlockSpec(m.shape, lambda i: (0, 0))
    edge = lambda at: pl.BlockSpec((3, BAND, lines, extent), lambda i: (0, at, i, 0))
    back = pl.BlockSpec((BAND, lines, extent), lambda i: (0, i, 0))
    shape = jax.ShapeDtypeStruct((BAND, shard_y, extent), jnp.float32)
    return pl.pallas_call(
        z_back_kernel,
        grid=(shard_y // lines,),
        in_specs=[whole(edge_low), whole(edge_high), edge(0), edge(last), edge(0), edge(0)],
        out_specs=[back, back],
        out_shape=[shape, shape],
        compiler_params=params(52 * 1024 * 1024),
        cost_estimate=cost(3e9, 2e7),
        name="z_back",
    )(edge_low, edge_high, velocity, velocity, halo_low, halo_high)


def combine_kernel(
    from_low, from_high, adjoint, carrier, tendency, halo_low, halo_high, stretch_y, out
):
    _, shard_z, group, extent = adjoint.shape
    rows = BAND * group
    top = shard_z - BAND
    for c in range(3):
        total = tendency[c]
        if c == 1:
            total = total - stretch_y[...]
        out[c] = adjoint[c] + STEP * total
        for matrix, halo, at in ((from_low, halo_low, 0), (from_high, halo_high, top)):
            part = apply_stacked(matrix[...], halo[c].reshape(rows, extent))
            planes = slice(at, at + BAND)
            out[c, planes] += STEP * (carrier[planes] * part.reshape(BAND, group, extent))


def combine(from_low, from_high, adjoint, velocity, tendency, halo_low, halo_high, stretch_y):
    _, shard_z, shard_y, extent = adjoint.shape
    whole = lambda m: pl.BlockSpec(m.shape, lambda i: (0, 0))
    block = pl.BlockSpec((3, shard_z, GROUP, extent), lambda i: (0, 0, i, 0))
    carrier = pl.BlockSpec((None, shard_z, GROUP, extent), lambda i: (2, 0, i, 0))
    halo = pl.BlockSpec((3, BAND, GROUP, extent), lambda i: (0, 0, i, 0))
    plane = pl.BlockSpec((shard_z, GROUP, extent), lambda i: (0, i, 0))
    return pl.pallas_call(
        combine_kernel,
        grid=(shard_y // GROUP,),
        in_specs=[whole(from_low), whole(from_high), block, carrier, block, halo, halo, plane],
        out_specs=block,
        out_shape=jax.ShapeDtypeStruct(adjoint.shape, jnp.float32),
        compiler_params=params(),
        cost_estimate=cost(3e9, 5e7),
        name="combine",
    )(from_low, from_high, adjoint, velocity, tendency, halo_low, halo_high, stretch_y)


def finish_kernel(back_low, back_high, updated, out):
    back = jnp.where(pl.program_id(0) == 0, back_low[...], back_high[...])
    out[...] = updated[...] - STEP * back


def finish(updated, back_low, back_high):
    _, shard_z, shard_y, extent = updated.shape
    last = shard_z // BAND - 1
    lines = shard_y // 2
    edge = pl.BlockSpec((None, BAND, lines, extent), lambda i, j: (2, i * last, j, 0))
    back = pl.BlockSpec((BAND, lines, extent), lambda i, j: (0, j, 0))
    return pl.pallas_call(
        finish_kernel,
        grid=(2, shard_y // lines),
        in_specs=[back, back, edge],
        out_specs=edge,
        out_shape=jax.ShapeDtypeStruct(updated.shape, jnp.float32),
        input_output_aliases={2: 0},
        compiler_params=params(8 * 1024 * 1024),
        cost_estimate=cost(1e6, 6e6),
        name="finish",
    )(back_low, back_high, updated)


def edges_kernel(last, count, adjoint, top, bottom, left, right):
    step = pl.program_id(0)
    left[...] = adjoint[:, :, adjoint.shape[2] - BY :]
    right[...] = adjoint[:, :, :BY]

    @pl.when(step < count)
    def _():
        bottom[...] = adjoint[...]

    @pl.when(step >= last)
    def _():
        top[...] = adjoint[...]


def edges(adjoint):
    parts, shard_z, shard_y, extent = adjoint.shape
    planes = 4
    count = BAND // planes
    steps = shard_z // planes
    last = steps - count
    plane_shape = jax.ShapeDtypeStruct((parts, BAND, shard_y, extent), jnp.float32)
    line_shape = jax.ShapeDtypeStruct((parts, shard_z, BY, extent), jnp.float32)
    block = (parts, planes, shard_y, extent)
    line = pl.BlockSpec((parts, planes, BY, extent), lambda i: (0, i, 0, 0))
    return pl.pallas_call(
        functools.partial(edges_kernel, last, count),
        grid=(steps,),
        in_specs=[pl.BlockSpec(block, lambda i: (0, i, 0, 0))],
        out_specs=[
            pl.BlockSpec(block, lambda i: (0, jnp.maximum(i - last, 0), 0, 0)),
            pl.BlockSpec(block, lambda i: (0, jnp.minimum(i, count - 1), 0, 0)),
            line,
            line,
        ],
        out_shape=[plane_shape, plane_shape, line_shape, line_shape],
        compiler_params=params(),
        cost_estimate=cost(1e6, 4e7),
        name="edges",
    )(adjoint)


def send_up(value, axis):
    size = lax.axis_size(axis)
    return lax.ppermute(value, axis, [(i, i + 1) for i in range(size - 1)])


def send_down(value, axis):
    size = lax.axis_size(axis)
    return lax.ppermute(value, axis, [(i + 1, i) for i in range(size - 1)])


def exchange(value, axis, distance):
    size = lax.axis_size(axis)
    return lax.ppermute(value, axis, [(i, i ^ distance) for i in range(size)])


def after(value, *others):
    return lax.optimization_barrier((value, *others))


def owner_rows(grad, turbine_owner):
    turbines = turbine_owner.shape[0]
    devices = lax.axis_size("wide") * lax.axis_size("narrow")
    slot_count = (turbines - 2) // devices + 2
    device = lax.axis_index("wide") * lax.axis_size("narrow") + lax.axis_index("narrow")
    positions = jnp.arange(turbines)
    shared = turbine_owner[:, None] == turbine_owner[None, :]
    earlier = positions[:, None] > positions[None, :]
    slot_rank = jnp.sum((shared & earlier).astype(jnp.int32), axis=1)
    mine = (turbine_owner[None, :] == device) & (jnp.arange(slot_count)[:, None] == slot_rank[None, :])
    return jnp.sum(jnp.where(mine[:, None, :], grad[None], 0.0), axis=2)


def on_device(
    adjoint, velocity, deriv_x, deriv_y, deriv_z, rotor_blocks, turbine_owner, disk_weight, thrust
):
    _, shard_z, shard_y, extent = adjoint.shape
    top, bottom, left, right = edges(adjoint)
    z_low = send_up(top, "wide")
    z_high = send_down(bottom, "wide")
    y_low = send_up(left, "narrow")
    y_high = send_down(right, "narrow")

    steps = [("narrow", 2**k) for k in range(8) if 2**k < lax.axis_size("narrow")]
    steps += [("wide", 2**k) for k in range(8) if 2**k < lax.axis_size("wide")]

    source, grad0, grad1 = turbine_terms(adjoint, velocity, rotor_blocks, disk_weight, thrust)
    scale = 1.0 / math.sqrt(128.0 * rotor_blocks.shape[1])
    grad = jnp.stack([jnp.sum(grad0, axis=1), jnp.sum(grad1, axis=1)]) * scale
    xy_matrices, z_pair, z_from, z_to = matrices(deriv_x, deriv_y, deriv_z, shard_z, shard_y)

    moved = exchange(grad, *steps[0])
    tendency = z_local(z_pair, adjoint, velocity)
    moved, tendency = after(moved, tendency)
    grad = grad + moved
    moved = exchange(grad, *steps[1])
    moved, y_low, y_high = after(moved, y_low, y_high)
    grad = grad + moved
    moved = exchange(grad, *steps[2])
    tendency, y_back_low, y_back_high = xy_terms(
        xy_matrices, adjoint, velocity, y_low, y_high, source, tendency
    )
    stretch_low = send_up(y_back_high, "narrow")
    stretch_high = send_down(y_back_low, "narrow")
    moved, tendency, z_low, z_high = after(moved, tendency, z_low, z_high)
    grad = grad + moved
    z_back_low, z_back_high = z_back(*z_to, velocity, z_low, z_high)
    last_low = send_up(z_back_high, "wide")
    last_high = send_down(z_back_low, "wide")
    moved = exchange(grad, *steps[3])
    rest = shard_y - BY
    stretch_y = jnp.pad(stretch_low, ((0, 0), (0, rest), (0, 0))) + jnp.pad(
        stretch_high, ((0, 0), (rest, 0), (0, 0))
    )
    updated = combine(*z_from, adjoint, velocity, tendency, z_low, z_high, stretch_y)
    moved, updated = after(moved, updated)
    grad = grad + moved
    for step in steps[4:]:
        grad = grad + exchange(grad, *step)
    return finish(updated, last_low, last_high), owner_rows(grad, turbine_owner)


def solution(mesh):
    return jax.shard_map(
        on_device,
        mesh=mesh,
        in_specs=(
            P(None, "wide", "narrow", None),
            P(None, "wide", "narrow", None),
            P(),
            P(),
            P(),
            P(),
            P(),
            P(),
            P(),
        ),
        out_specs=(P(None, "wide", "narrow", None), P(("wide", "narrow"), None)),
        check_vma=False,
    )
```
